128 devices in a mesh: dp: 2 (over core), seq: 64 (over x, z, y).
Axes of the slice: x: 4, y: 4, z: 4, core: 2. Of those that a mesh axis runs over, the one named last changes fastest.
Arguments:
- queries: bfloat16 [2, 32768, 1024], P('dp', 'seq'), may hold values from -16 to 16
- keys: bfloat16 [2, 32768, 1024], P('dp', 'seq'), may hold values from -16 to 16
- values: bfloat16 [2, 32768, 1024], P('dp', 'seq'), may hold values from -6 to 6
- offsets: int32 [8], replicated, may hold values from 0 to 15, as said below
- out_weight: bfloat16 [1024, 2048], replicated, may hold values from -0.1875 to 0.1875
- grad_out: bfloat16 [2, 32768, 2048], P('dp', 'seq'), may hold values from -16 to 16
Outputs:
- result: bfloat16 [2, 32768, 2048], P('dp', 'seq')
- grad_queries: bfloat16 [2, 32768, 1024], P('dp', 'seq')
- grad_keys: bfloat16 [2, 32768, 1024], P('dp', 'seq')
- grad_values: bfloat16 [2, 32768, 1024], P('dp', 'seq')
- weight_grad: float32 [1024, 2048], replicated
The draws below stay inside these ranges and needn't reach their ends.
Inputs may be any that keep to these rules, and one draw needn't show every extreme that they name: offsets[h] is the residue mod 16 of head h's dilated positions.
All inputs are finite; a program needn't handle non-finite values.
Results may differ from the reference program's by a relative error of at most 0.017.
Values may be sent and summed in bfloat16 or wider, within the bound.
A program may use at most 192 MiB of HBM per device.

```python
import math
import jax
import jax.numpy as jnp
from jax import lax

D = 2048
HEADS = 8
HEAD_DIM = 128
RATE = 16
TOK_DEV = 512
REPLICAS = 2
TOKENS = 32768


def head_offsets(key):
    order = jax.random.permutation(jax.random.fold_in(key, 11), HEADS)
    middle = jax.random.randint(jax.random.fold_in(key, 12), (HEADS,), 1, RATE - 1)
    return jnp.where(order == 0, 0, jnp.where(order == 1, RATE - 1, middle)).astype(jnp.int32)


def draw_offsets(key, part):
    return head_offsets(key)


def draw_queries(key, part):
    key = jax.random.fold_in(key, 3)
    shape = (REPLICAS, TOKENS, HEADS * HEAD_DIM)
    result_rows = 1.5 * jax.random.normal(key, shape, jnp.float32)
    return jnp.clip(result_rows, -16.0, 16.0).astype(jnp.bfloat16)


def draw_keys(key, part):
    key = jax.random.fold_in(key, 5)
    shape = (REPLICAS, TOKENS, HEADS * HEAD_DIM)
    result_rows = 1.5 * jax.random.normal(key, shape, jnp.float32)
    return jnp.clip(result_rows, -16.0, 16.0).astype(jnp.bfloat16)


def raised(values, stream_key, source, target, parts, factor):
    owner, partner = [(jnp.arange(values.shape[axis_at]) // (values.shape[axis_at] // parts)).reshape([-1 if axis == axis_at else 1 for axis in range(values.ndim)]) for axis_at in (source, target)]
    chosen = jax.random.permutation(stream_key, parts)[partner]
    strong = (owner == chosen) | (owner == (partner + parts // 2) % parts)
    return jnp.where(strong, factor * values, values)


def shard_levels(stream_key, extent, cuts, least, top_value):
    factor_of = 1.0
    for dim, shards_of in cuts:
        heights = jax.random.uniform(jax.random.fold_in(jax.random.fold_in(stream_key, 6), dim), (shards_of,), jnp.float32, least / len(cuts), top_value / len(cuts))
        factor_of = factor_of * jnp.repeat(jnp.exp(heights), extent[dim] // shards_of).reshape((-1,) + (1,) * (len(extent) - 1 - dim))
    return factor_of


def gaussian(stream_key, shape, deviation, most, split=(), held_as=jnp.bfloat16):
    result = deviation * jax.random.normal(stream_key, shape, jnp.float32)
    if split:
        result = result * shard_levels(stream_key, shape, split, -0.22, 0.18)
    return jnp.clip(result, -most, most).astype(held_as)


def bell_draw_with(stream_key, dims, width, reach, pieces, heavy, kind=jnp.bfloat16):
    result = width * jax.random.normal(stream_key, dims, jnp.float32)
    if pieces:
        result = result * shard_levels(stream_key, dims, pieces, -0.22, 0.18)
    return jnp.clip(raised(result, jax.random.fold_in(stream_key, 3), *heavy), -reach, reach).astype(kind)


def setup_inputs(seed: int = 0) -> dict:
    splits = jax.random.split(jax.random.key(seed), 7)
    return {
        "queries": draw_queries(jax.random.fold_in(splits[6], 71), 0),
        "keys": draw_keys(jax.random.fold_in(splits[6], 71), 0),
        "values": gaussian(splits[2], (REPLICAS, TOKENS, HEADS * HEAD_DIM), 1.0, 6.0, ((0, 2), (1, 64))),
        "offsets": draw_offsets(jax.random.fold_in(splits[6], 71), 0),
        "out_weight": gaussian(splits[4], (HEADS * HEAD_DIM, D), (HEADS * HEAD_DIM) ** -0.5, 0.1875),
        "grad_out": bell_draw_with(splits[5], (REPLICAS, TOKENS, D), 1.0, 16.0, ((0, 2), (1, 64)), (1, 2, 64, 4.0)),
    }


def near_forward(query_block, key_block, value_block, score_scale):
    scores = jnp.einsum('ihe,jhe->hij', query_block.astype(jnp.float32), key_block.astype(jnp.float32)) * score_scale
    lse_block = jax.nn.logsumexp(scores, axis=2)
    weights = jnp.exp(scores - lse_block[:, :, None]).astype(jnp.bfloat16)
    out_block = jnp.einsum('hij,jhe->ihe', weights.astype(jnp.float32), value_block.astype(jnp.float32))
    return (lse_block.T, out_block)

def near_backward(query_block, key_block, value_block, lse_block, delta_block, grad_block, score_scale):
    scores = jnp.einsum('ihe,jhe->hij', query_block.astype(jnp.float32), key_block.astype(jnp.float32)) * score_scale
    probs = jnp.exp(scores - lse_block.T[:, :, None])
    probs_low = probs.astype(jnp.bfloat16).astype(jnp.float32)
    grad_float = grad_block.astype(jnp.float32)
    value_gradient = jnp.einsum('hij,ihe->jhe', probs_low, grad_float)
    dprob = jnp.einsum('ihe,jhe->hij', grad_float, value_block.astype(jnp.float32))
    dscore = (probs * (dprob - delta_block.T[:, :, None])).astype(jnp.bfloat16).astype(jnp.float32)
    query_gradient = jnp.einsum('hij,jhe->ihe', dscore, key_block.astype(jnp.float32)) * score_scale
    key_gradient = jnp.einsum('hij,ihe->jhe', dscore, query_block.astype(jnp.float32)) * score_scale
    return (query_gradient, key_gradient, value_gradient)

def far_forward(query_rows, key_rows, value_rows, score_scale):
    scores = jnp.dot(query_rows, key_rows.T, preferred_element_type=jnp.float32) * score_scale
    lse_rows = jax.nn.logsumexp(scores, axis=1)
    weights = jnp.exp(scores - lse_rows[:, None]).astype(jnp.bfloat16)
    return (lse_rows, jnp.dot(weights, value_rows, preferred_element_type=jnp.float32))

def far_backward(query_rows, key_rows, value_rows, lse_rows, delta_rows, grad_rows, score_scale):
    scores = jnp.dot(query_rows, key_rows.T, preferred_element_type=jnp.float32) * score_scale
    probs = jnp.exp(scores - lse_rows[:, None])
    value_gradient = jnp.dot(probs.astype(jnp.bfloat16).T, grad_rows, preferred_element_type=jnp.float32)
    dprob = jnp.dot(grad_rows, value_rows.T, preferred_element_type=jnp.float32)
    dscore = (probs * (dprob - delta_rows[:, None])).astype(jnp.bfloat16)
    query_gradient = jnp.dot(dscore, key_rows, preferred_element_type=jnp.float32) * score_scale
    key_gradient = jnp.dot(dscore.T, query_rows, preferred_element_type=jnp.float32) * score_scale
    return (query_gradient, key_gradient, value_gradient)

def reference(queries, keys, values, offsets, out_weight, grad_out):
    score_scale = HEAD_DIM ** (-0.5)
    far_count = TOKENS // RATE
    block_count = TOKENS // TOK_DEV
    weight_total = jnp.zeros((HEADS * HEAD_DIM, D), jnp.float32)
    results, query_grads, key_grads, value_grads = ([], [], [], [])
    for replica in range(REPLICAS):
        query_per_head = queries[replica].reshape(TOKENS, HEADS, HEAD_DIM)
        key_per_head = keys[replica].reshape(TOKENS, HEADS, HEAD_DIM)
        value_per_head = values[replica].reshape(TOKENS, HEADS, HEAD_DIM)
        blocked = tuple((t.reshape(block_count, TOK_DEV, HEADS, HEAD_DIM) for t in (query_per_head, key_per_head, value_per_head)))
        near_lse, local_output = lax.map(lambda trio: near_forward(trio[0], trio[1], trio[2], score_scale), blocked)
        near_lse = near_lse.reshape(TOKENS, HEADS)
        local_output = local_output.reshape(TOKENS, HEADS, HEAD_DIM)
        mixed_lse, mixed_out = (near_lse, local_output)
        dilated_sets = []
        for head_index in range(HEADS):
            positions = (offsets[head_index] + RATE * jnp.arange(far_count, dtype=jnp.int32)).astype(jnp.int32)
            query_rows = jnp.take(query_per_head[:, head_index], positions, axis=0)
            key_rows = jnp.take(key_per_head[:, head_index], positions, axis=0)
            value_rows = jnp.take(value_per_head[:, head_index], positions, axis=0)
            far_lse, far_out = far_forward(query_rows, key_rows, value_rows, score_scale)
            near_part = near_lse[positions, head_index]
            merged = jnp.logaddexp(near_part, far_lse)
            blended = jnp.exp(near_part - merged)[:, None] * local_output[positions, head_index] + jnp.exp(far_lse - merged)[:, None] * far_out
            mixed_lse = mixed_lse.at[positions, head_index].set(merged)
            mixed_out = mixed_out.at[positions, head_index].set(blended)
            dilated_sets.append((positions, query_rows, key_rows, value_rows))
        attended = mixed_out.astype(jnp.bfloat16)
        flat = attended.reshape(TOKENS, HEADS * HEAD_DIM)
        results.append(jnp.dot(flat, out_weight, preferred_element_type=jnp.float32).astype(jnp.bfloat16))
        grad_rows_all = grad_out[replica]
        weight_total = weight_total + jnp.dot(flat.T, grad_rows_all, preferred_element_type=jnp.float32)
        grad_attended = jnp.dot(grad_rows_all, out_weight.T, preferred_element_type=jnp.float32).astype(jnp.bfloat16)
        gradient_per_head = grad_attended.reshape(TOKENS, HEADS, HEAD_DIM)
        output_gradient_dot = lax.optimization_barrier(jnp.sum(gradient_per_head.astype(jnp.float32) * attended.astype(jnp.float32), axis=2))
        inputs = blocked + (mixed_lse.reshape(block_count, TOK_DEV, HEADS), output_gradient_dot.reshape(block_count, TOK_DEV, HEADS), gradient_per_head.reshape(block_count, TOK_DEV, HEADS, HEAD_DIM))
        query_gradient, key_gradient, value_gradient = lax.map(lambda six: near_backward(six[0], six[1], six[2], six[3], six[4], six[5], score_scale), inputs)
        query_gradient = query_gradient.reshape(TOKENS, HEADS, HEAD_DIM)
        key_gradient = key_gradient.reshape(TOKENS, HEADS, HEAD_DIM)
        value_gradient = value_gradient.reshape(TOKENS, HEADS, HEAD_DIM)
        for head_index in range(HEADS):
            positions, query_rows, key_rows, value_rows = dilated_sets[head_index]
            far_q, far_k, far_v = far_backward(query_rows, key_rows, value_rows, mixed_lse[positions, head_index], output_gradient_dot[positions, head_index], gradient_per_head[positions, head_index], score_scale)
            query_gradient = query_gradient.at[positions, head_index].add(far_q)
            key_gradient = key_gradient.at[positions, head_index].add(far_k)
            value_gradient = value_gradient.at[positions, head_index].add(far_v)
        query_grads.append(query_gradient.reshape(TOKENS, HEADS * HEAD_DIM).astype(jnp.bfloat16))
        key_grads.append(key_gradient.reshape(TOKENS, HEADS * HEAD_DIM).astype(jnp.bfloat16))
        value_grads.append(value_gradient.reshape(TOKENS, HEADS * HEAD_DIM).astype(jnp.bfloat16))
    weight_grad = weight_total * (1.0 / math.sqrt(REPLICAS * TOKENS))
    return (jnp.stack(results), jnp.stack(query_grads), jnp.stack(key_grads), jnp.stack(value_grads), weight_grad)
```

```python
import math

import jax
import jax.numpy as jnp
from jax import lax
from jax.experimental import pallas as pl
from jax.experimental.pallas import tpu as pltpu
from jax.sharding import PartitionSpec as P

RATE = 16
MESH = pl.DeviceIdType.MESH

STRIDES = (16, 4, 1)
ORDERS = ((0, 1, 2), (1, 2, 0), (2, 0, 1))
WIDTHS = (384, 384, 384, 384, 256, 256)
STARTS = (0, 384, 768, 1152, 1536, 1792)
PARTS = [(ORDERS[p % 3], p // 3) for p in range(6)]
STEP_ROWS = (256, 128, 64, 32)
STEP_OFF = (0, 256, 384, 448)


def ar_kernel(flat_ref, grad_ref, out_ref, flat_t, acc, sbuf, rbuf, s0, r0, last, send_sem, recv_sem):
    dp = lax.axis_index("dp")
    seq = lax.axis_index("seq")
    coord = [(seq // st) % 4 for st in STRIDES]

    def peer(axis, c):
        return (dp, seq + (c - coord[axis]) * STRIDES[axis])

    sibling = (1 - dp, seq)
    barrier = pltpu.get_barrier_semaphore()
    pl.semaphore_signal(barrier, inc=1, device_id=sibling, device_id_type=MESH)
    for axis in range(3):
        for d in (1, 2, 3):
            pl.semaphore_signal(barrier, inc=1, device_id=peer(axis, (coord[axis] + d) % 4), device_id_type=MESH)
    flat_t[...] = flat_ref[...].T
    mine = pl.multiple_of(dp * 512, 512)
    other = pl.multiple_of((1 - dp) * 512, 512)

    def copy(p, k, src, dst, target):
        return pltpu.make_async_remote_copy(src_ref=src, dst_ref=dst, send_sem=send_sem.at[p, k], recv_sem=recv_sem.at[p, k], device_id=target, device_id_type=MESH)

    cols = [slice(STARTS[p], STARTS[p] + WIDTHS[p]) for p in range(6)]
    started = []
    first = []
    for p in range(6):
        s0[:, cols[p]] = jnp.dot(flat_t[pl.ds(other, 512), :], grad_ref[:, cols[p]], preferred_element_type=jnp.float32).astype(jnp.bfloat16)
        if p == 0:
            pl.semaphore_wait(barrier, 10)
        c = copy(p, 0, s0.at[:, cols[p]], r0.at[:, cols[p]], sibling)
        c.start()
        first.append(c)
    started += first
    for p in range(6):
        acc[:, cols[p]] = jnp.dot(flat_t[pl.ds(mine, 512), :], grad_ref[:, cols[p]], preferred_element_type=jnp.float32)

    base = [0] * 6
    flight = [None] * 6
    history = [[] for _ in range(6)]

    def launch(p, s):
        order, swap = PARTS[p]
        axis = order[s // 2]
        c = coord[axis]
        use_a = (s % 2) == swap
        if use_a:
            bit, target = ((c + 1) // 2) % 2, peer(axis, c + 1 - 2 * (c % 2))
        else:
            bit, target = c // 2, peer(axis, 3 - c)
        n = STEP_ROWS[s]
        keep = pl.multiple_of(base[p] + bit * n, n)
        send = pl.multiple_of(base[p] + (1 - bit) * n, n)
        rows = slice(STEP_OFF[s], STEP_OFF[s] + n)
        sbuf[rows, cols[p]] = acc[pl.ds(send, n), cols[p]].astype(jnp.bfloat16)
        cp = copy(p, 1 + s, sbuf.at[rows, cols[p]], rbuf.at[rows, cols[p]], target)
        cp.start()
        started.append(cp)
        history[p].append((keep, send, target))
        base[p] = keep
        flight[p] = cp

    for p in range(6):
        first[p].wait_recv()
        acc[:, cols[p]] += r0[:, cols[p]].astype(jnp.float32)
        launch(p, 0)
    lasts = [None] * 6
    for s in range(4):
        n = STEP_ROWS[s]
        rows = slice(STEP_OFF[s], STEP_OFF[s] + n)
        for p in range(6):
            flight[p].wait_recv()
            acc[pl.ds(base[p], n), cols[p]] += rbuf[rows, cols[p]].astype(jnp.float32)
            if s < 3:
                launch(p, s + 1)
            else:
                order, _ = PARTS[p]
                axis = order[2]
                sbuf[480:512, cols[p]] = acc[pl.ds(base[p], 32), cols[p]].astype(jnp.bfloat16)
                lasts[p] = []
                for d in (1, 2, 3):
                    cp = copy(p, 4 + d, sbuf.at[480:512, cols[p]], last.at[d - 1, :, cols[p]], peer(axis, (coord[axis] + d) % 4))
                    cp.start()
                    started.append(cp)
                    lasts[p].append(cp)
    gather = [None] * 6
    for p in range(6):
        total = acc[pl.ds(base[p], 32), cols[p]]
        axis = PARTS[p][0][2]
        for d in (1, 2, 3):
            lasts[p][d - 1].wait_recv()
        total = sbuf[480:512, cols[p]].astype(jnp.float32)
        for d in (1, 2, 3):
            total = total + last[d - 1, :, cols[p]].astype(jnp.float32)
        here = out_ref.at[pl.ds(pl.multiple_of(mine + base[p], 32), 32), cols[p]]
        out_ref[pl.ds(pl.multiple_of(mine + base[p], 32), 32), cols[p]] = total.astype(jnp.bfloat16)
        cp = copy(p, 8, here, here, history[p][3][2])
        cp.start()
        started.append(cp)
        gather[p] = cp
    for s in (3, 2, 1, 0):
        for p in range(6):
            gather[p].wait_recv()
            keep, send, _ = history[p][s]
            n = STEP_ROWS[s]
            low = keep if s == 4 else None
            if s > 0:
                start = pl.multiple_of(mine + history[p][s - 1][0], 2 * n)
                here = out_ref.at[pl.ds(start, 2 * n), cols[p]]
                cp = copy(p, 12 - s, here, here, history[p][s - 1][2])
                cp.start()
                started.append(cp)
                gather[p] = cp
                if s == 1:
                    cp = copy(p, 12, here, here, sibling)
                    cp.start()
                    started.append(cp)
                    history[p].append(cp)
            else:
                start = pl.multiple_of(mine + history[p][0][1], n)
                here = out_ref.at[pl.ds(start, n), cols[p]]
                cp = copy(p, 13, here, here, sibling)
                cp.start()
                started.append(cp)
                history[p].append(cp)
    for p in range(6):
        history[p][-1].wait_recv()
        history[p][-2].wait_recv()
    for cp in started:
        cp.wait_send()


def all_reduce_term(flat, grad):
    return pl.pallas_call(
        ar_kernel,
        out_shape=jax.ShapeDtypeStruct((1024, 2048), jnp.bfloat16),
        in_specs=[pl.BlockSpec(memory_space=pltpu.VMEM)] * 2,
        out_specs=pl.BlockSpec(memory_space=pltpu.VMEM),
        scratch_shapes=[
            pltpu.VMEM((1024, 512), jnp.bfloat16),
            pltpu.VMEM((512, 2048), jnp.float32),
            pltpu.VMEM((512, 2048), jnp.bfloat16),
            pltpu.VMEM((512, 2048), jnp.bfloat16),
            pltpu.VMEM((512, 2048), jnp.bfloat16),
            pltpu.VMEM((512, 2048), jnp.bfloat16),
            pltpu.VMEM((3, 32, 2048), jnp.bfloat16),
            pltpu.SemaphoreType.DMA((6, 14)),
            pltpu.SemaphoreType.DMA((6, 14)),
        ],
        compiler_params=pltpu.CompilerParams(collective_id=0, has_side_effects=True, vmem_limit_bytes=60 * 1024 * 1024),
    )(flat, grad)


def select_rows(source, selected_rows):
    dilation, number_of_heads = selected_rows.shape
    grouped = source.reshape((source.shape[0] // dilation, dilation) + source.shape[1:])
    slot_mask = selected_rows.reshape((1, dilation, number_of_heads) + (1,) * (source.ndim - 2))
    return jnp.sum(jnp.where(slot_mask, grouped, jnp.zeros((), source.dtype)), axis=1)


def deposit_rows(picked, selected_rows):
    dilation, number_of_heads = selected_rows.shape
    slot_mask = selected_rows.reshape((1, dilation, number_of_heads) + (1,) * (picked.ndim - 2))
    widened = jnp.where(slot_mask, picked[:, None], jnp.zeros((), picked.dtype))
    return widened.reshape((picked.shape[0] * dilation,) + picked.shape[1:])


def sent_to_holder(source, holder_replica_group):
    leading = jnp.moveaxis(source, 1, 0)[:, None]
    padding = jnp.zeros(
        (leading.shape[0], holder_replica_group - 1) + leading.shape[2:], source.dtype
    )
    joined = jnp.concatenate([leading, padding], axis=1)
    return joined.reshape((leading.shape[0] * holder_replica_group,) + leading.shape[2:])


def received_from_holder(source, number_of_heads, holder_replica_group):
    picked = source.reshape((number_of_heads, holder_replica_group) + source.shape[1:])[:, 0]
    return jnp.moveaxis(picked, 0, 1)


def per_device(queries, keys, values, offsets, out_weight, grad_out):
    row_count = queries.shape[1]
    number_of_heads = offsets.shape[0]
    head_depth = queries.shape[2] // number_of_heads
    score_scale = head_depth ** (-0.5)
    dilation = RATE
    dilated_count = row_count // dilation
    seq_count = lax.axis_size("seq")
    holder_replica_group = seq_count // number_of_heads
    far_total = seq_count * dilated_count
    slot_ids = jnp.arange(dilation, dtype=jnp.int32)
    selected_rows = offsets[None, :] == slot_ids[:, None]
    dilated_mask = jnp.broadcast_to(
        selected_rows[None], (dilated_count, dilation, number_of_heads)
    ).reshape(row_count, number_of_heads)
    query_per_head = queries[0].reshape(row_count, number_of_heads, head_depth)
    key_per_head = keys[0].reshape(row_count, number_of_heads, head_depth)
    value_per_head = values[0].reshape(row_count, number_of_heads, head_depth)
    near_scores = (
        jnp.einsum("ihe,jhe->hij", query_per_head, key_per_head, preferred_element_type=jnp.float32)
        * score_scale
    )
    near_lse = jax.nn.logsumexp(near_scores, axis=2)
    near_weights = jnp.exp(near_scores - near_lse[:, :, None]).astype(jnp.bfloat16)
    local_output = jnp.einsum(
        "hij,jhe->ihe", near_weights, value_per_head, preferred_element_type=jnp.float32
    )
    sparse_query_rows = select_rows(query_per_head, selected_rows)
    sparse_key_rows = select_rows(key_per_head, selected_rows)
    sparse_value_rows = select_rows(value_per_head, selected_rows)
    got_query, got_key, got_value = (
        lax.all_to_all(
            sent_to_holder(sparse_query_rows, holder_replica_group),
            "seq",
            split_axis=0,
            concat_axis=0,
            tiled=True,
        ),
        lax.all_to_all(
            sent_to_holder(sparse_key_rows, holder_replica_group),
            "seq",
            split_axis=0,
            concat_axis=0,
            tiled=True,
        ),
        lax.all_to_all(
            sent_to_holder(sparse_value_rows, holder_replica_group),
            "seq",
            split_axis=0,
            concat_axis=0,
            tiled=True,
        ),
    )
    owner_query = got_query.reshape(far_total, head_depth)
    owner_key = got_key.reshape(far_total, head_depth)
    owner_value = got_value.reshape(far_total, head_depth)
    far_scores = (
        jnp.einsum("me,ne->mn", owner_query, owner_key, preferred_element_type=jnp.float32)
        * score_scale
    )
    far_lse = jax.nn.logsumexp(far_scores, axis=1)
    far_weights = jnp.exp(far_scores - far_lse[:, None]).astype(jnp.bfloat16)
    far_out = jnp.dot(far_weights, owner_value, preferred_element_type=jnp.float32)
    returned_output_rows, returned_log_normalizer = (
        lax.all_to_all(
            far_out.reshape(seq_count, dilated_count, head_depth),
            "seq",
            split_axis=0,
            concat_axis=0,
            tiled=True,
        ),
        lax.all_to_all(
            far_lse.reshape(seq_count, dilated_count),
            "seq",
            split_axis=0,
            concat_axis=0,
            tiled=True,
        ),
    )
    sparse_output = received_from_holder(
        returned_output_rows, number_of_heads, holder_replica_group
    )
    sparse_log_normalizer = received_from_holder(
        returned_log_normalizer, number_of_heads, holder_replica_group
    )
    local_row_log_normalizer = near_lse.T
    local_sparse_log_normalizer = select_rows(local_row_log_normalizer, selected_rows)
    local_sparse_output = select_rows(local_output, selected_rows)
    upper_limit = jnp.maximum(local_sparse_log_normalizer, sparse_log_normalizer)
    combined_log_normalizer = upper_limit + jnp.log(
        jnp.exp(local_sparse_log_normalizer - upper_limit)
        + jnp.exp(sparse_log_normalizer - upper_limit)
    )
    blended = (
        jnp.exp(local_sparse_log_normalizer - combined_log_normalizer)[:, :, None]
        * local_sparse_output
        + jnp.exp(sparse_log_normalizer - combined_log_normalizer)[:, :, None] * sparse_output
    )
    mixed_lse = jnp.where(
        dilated_mask, deposit_rows(combined_log_normalizer, selected_rows), local_row_log_normalizer
    )
    attended = jnp.where(
        dilated_mask[:, :, None], deposit_rows(blended, selected_rows), local_output
    ).astype(jnp.bfloat16)
    flat = attended.reshape(row_count, number_of_heads * head_depth)
    result = jnp.dot(flat, out_weight, preferred_element_type=jnp.float32).astype(jnp.bfloat16)
    grad_rows = grad_out[0]
    grad_flat = lax.dot_general(
        grad_rows, out_weight, (((1,), (1,)), ((), ())), preferred_element_type=jnp.float32
    ).astype(jnp.bfloat16)
    gradient_per_head = grad_flat.reshape(row_count, number_of_heads, head_depth)
    output_gradient_dot = jnp.sum(
        gradient_per_head.astype(jnp.float32) * attended.astype(jnp.float32), axis=2
    )
    near_probs = jnp.exp(near_scores - mixed_lse.T[:, :, None])
    local_value_gradient = jnp.einsum(
        "hij,ihe->jhe",
        near_probs.astype(jnp.bfloat16),
        gradient_per_head,
        preferred_element_type=jnp.float32,
    )
    near_dprob = jnp.einsum(
        "ihe,jhe->hij", gradient_per_head, value_per_head, preferred_element_type=jnp.float32
    )
    near_dscore = (near_probs * (near_dprob - output_gradient_dot.T[:, :, None])).astype(
        jnp.bfloat16
    )
    local_query_gradient = (
        jnp.einsum("hij,jhe->ihe", near_dscore, key_per_head, preferred_element_type=jnp.float32)
        * score_scale
    )
    local_key_gradient = (
        jnp.einsum("hij,ihe->jhe", near_dscore, query_per_head, preferred_element_type=jnp.float32)
        * score_scale
    )
    sparse_output_gradient = select_rows(gradient_per_head, selected_rows)
    sparse_gradient_dot = select_rows(output_gradient_dot, selected_rows)
    sent_grad, sent_lse, sent_delta = (
        lax.all_to_all(
            sent_to_holder(sparse_output_gradient.astype(jnp.float32), holder_replica_group),
            "seq",
            split_axis=0,
            concat_axis=0,
            tiled=True,
        ),
        lax.all_to_all(
            sent_to_holder(combined_log_normalizer, holder_replica_group),
            "seq",
            split_axis=0,
            concat_axis=0,
            tiled=True,
        ),
        lax.all_to_all(
            sent_to_holder(sparse_gradient_dot, holder_replica_group),
            "seq",
            split_axis=0,
            concat_axis=0,
            tiled=True,
        ),
    )
    owner_grad = sent_grad.reshape(far_total, head_depth).astype(jnp.bfloat16)
    owner_lse = sent_lse.reshape(far_total)
    owner_delta = sent_delta.reshape(far_total)
    far_probs = jnp.exp(far_scores - owner_lse[:, None])
    far_value_grad = jnp.einsum(
        "mn,me->ne", far_probs.astype(jnp.bfloat16), owner_grad, preferred_element_type=jnp.float32
    )
    far_dprob = jnp.einsum("me,ne->mn", owner_grad, owner_value, preferred_element_type=jnp.float32)
    far_dscore = (far_probs * (far_dprob - owner_delta[:, None])).astype(jnp.bfloat16)
    far_query_grad = (
        jnp.dot(far_dscore, owner_key, preferred_element_type=jnp.float32) * score_scale
    )
    far_key_grad = (
        jnp.einsum("mn,me->ne", far_dscore, owner_query, preferred_element_type=jnp.float32)
        * score_scale
    )
    returned_query_rows, returned_key_rows, returned_value_rows = (
        lax.all_to_all(
            far_query_grad.reshape(seq_count, dilated_count, head_depth).astype(jnp.bfloat16),
            "seq",
            split_axis=0,
            concat_axis=0,
            tiled=True,
        ).astype(jnp.float32),
        lax.all_to_all(
            far_key_grad.reshape(seq_count, dilated_count, head_depth).astype(jnp.bfloat16),
            "seq",
            split_axis=0,
            concat_axis=0,
            tiled=True,
        ).astype(jnp.float32),
        lax.all_to_all(
            far_value_grad.reshape(seq_count, dilated_count, head_depth).astype(jnp.bfloat16),
            "seq",
            split_axis=0,
            concat_axis=0,
            tiled=True,
        ).astype(jnp.float32),
    )
    sparse_query_gradient = received_from_holder(
        returned_query_rows, number_of_heads, holder_replica_group
    )
    sparse_key_gradient = received_from_holder(
        returned_key_rows, number_of_heads, holder_replica_group
    )
    sparse_value_gradient = received_from_holder(
        returned_value_rows, number_of_heads, holder_replica_group
    )
    query_gradient = (
        local_query_gradient + deposit_rows(sparse_query_gradient, selected_rows)
    ).astype(jnp.bfloat16)
    key_gradient = (local_key_gradient + deposit_rows(sparse_key_gradient, selected_rows)).astype(
        jnp.bfloat16
    )
    value_gradient = (
        local_value_gradient + deposit_rows(sparse_value_gradient, selected_rows)
    ).astype(jnp.bfloat16)
    weight_total = all_reduce_term(flat, grad_rows).astype(jnp.float32)
    token_total = row_count * seq_count * lax.axis_size("dp")
    weight_grad = weight_total * (1.0 / math.sqrt(token_total))
    flat_width = number_of_heads * head_depth
    return (
        result[None],
        query_gradient.reshape(1, row_count, flat_width),
        key_gradient.reshape(1, row_count, flat_width),
        value_gradient.reshape(1, row_count, flat_width),
        weight_grad,
    )


def solution(mesh):
    in_specs = (
        P("dp", "seq", None),
        P("dp", "seq", None),
        P("dp", "seq", None),
        P(),
        P(),
        P("dp", "seq", None),
    )
    out_specs = (
        P("dp", "seq", None),
        P("dp", "seq", None),
        P("dp", "seq", None),
        P("dp", "seq", None),
        P(),
    )
    return jax.shard_map(
        per_device, mesh=mesh, in_specs=in_specs, out_specs=out_specs, check_vma=False
    )
```

```python
import math

import jax
import jax.numpy as jnp
from jax import lax
from jax.experimental import pallas as pl
from jax.experimental.pallas import tpu as pltpu
from jax.sharding import PartitionSpec as P
MESH = pl.DeviceIdType.MESH

RATE = 16
HEADS = 8
DIM = 128
TOK = 512
PICK = 32
HOLD = 8
SCALE = DIM ** -0.5
LOG2E = math.log2(math.e)
SCALE2 = SCALE * LOG2E
NT = (((1,), (1,)), ((), ()))
TN = (((0,), (0,)), ((), ()))


def mm(a, b, dims=(((1,), (0,)), ((), ()))):
    return lax.dot_general(a, b, dims, preferred_element_type=jnp.float32)


def head_cols(h):
    return pl.ds(pl.multiple_of(h * DIM, DIM), DIM)


def picker(off):
    row = lax.broadcasted_iota(jnp.int32, (PICK, TOK), 0)
    pos = lax.broadcasted_iota(jnp.int32, (PICK, TOK), 1)
    return pos == row * RATE + off


def with_ones(value):
    return jnp.concatenate([value, jnp.ones_like(value)], axis=1)


def softmax_out(q, k, v1):
    s = mm(q, k, NT)
    top = jnp.max(s, axis=1, keepdims=True) * SCALE2
    e = jnp.exp2(s * SCALE2 - top).astype(jnp.bfloat16)
    ov = mm(e, v1)
    total = ov[:, DIM:]
    return ov[:, :DIM] / total, top + jnp.log(total) * LOG2E


def wait_bytes(ref, sem):
    pltpu.make_async_copy(ref, ref, sem).wait()


def far_kernel(off_ref, q_ref, k_ref, v_ref, w_hbm, grad_hbm,
               att_ref, g_ref, lse_ref, delta_ref, dkv_ref, dq_ref,
               w_ref, grad_ref, kv_sel, q_sel, g_sel, os_sel, kv_all, q_all, g_all, os_all,
               back_att, back_stat, got_att, got_stat, near_out, lse_cols, dq_acc,
               load_sem, send_sem, recv_sem):
    dp = lax.axis_index("dp")
    seq = lax.axis_index("seq")
    my_head, my_part = seq // HOLD, seq % HOLD
    load_w = pltpu.make_async_copy(w_hbm, w_ref, load_sem.at[0])
    load_g = pltpu.make_async_copy(grad_hbm, grad_ref, load_sem.at[1])
    load_w.start()
    load_g.start()
    barrier = pltpu.get_barrier_semaphore()

    @pl.loop(1, 64)
    def _(i):
        pl.semaphore_signal(barrier, inc=1, device_id=(dp, lax.rem(seq + i, 64)), device_id_type=MESH)

    @pl.loop(0, HEADS)
    def _(h):
        s = picker(off_ref[h]).astype(jnp.bfloat16)
        kv_sel[h, 0] = mm(s, k_ref[:, head_cols(h)]).astype(jnp.bfloat16)
        kv_sel[h, 1] = mm(s, v_ref[:, head_cols(h)]).astype(jnp.bfloat16)
        q_sel[h] = mm(s, q_ref[:, head_cols(h)]).astype(jnp.bfloat16)

    pl.semaphore_wait(barrier, 63)

    @pl.loop(1, 64)
    def _(i):
        d = lax.rem(seq + i, 64)
        pltpu.make_async_remote_copy(
            src_ref=kv_sel.at[d // HOLD], dst_ref=kv_all.at[:, seq], send_sem=send_sem.at[0], recv_sem=recv_sem.at[0],
            device_id=(dp, d), device_id_type=MESH).start()

    kv_all[:, seq] = kv_sel[my_head]

    def to_group(src, dst, k):
        @pl.loop(1, HEADS)
        def _(i):
            h = lax.rem(my_head + i, HEADS)
            pltpu.make_async_remote_copy(
                src_ref=src.at[h], dst_ref=dst.at[my_head], send_sem=send_sem.at[k], recv_sem=recv_sem.at[k],
                device_id=(dp, h * HOLD + my_part), device_id_type=MESH).start()
        dst[my_head] = src[my_head]

    to_group(q_sel, q_all, 1)

    @pl.loop(0, HEADS)
    def _(h):
        o, lse = softmax_out(q_sel[h], k_ref[:, head_cols(h)], with_ones(v_ref[:, head_cols(h)]))
        os_sel[h, 0] = o
        os_sel[h, 1] = lse

    to_group(os_sel, os_all, 2)
    load_w.wait()
    load_g.wait()

    @pl.loop(0, 4)
    def _(c):
        cols = pl.ds(pl.multiple_of(c * 256, 256), 256)
        g_ref[:, cols] = mm(grad_ref[...], w_ref[cols, :], NT).astype(jnp.bfloat16)

    @pl.loop(0, HEADS)
    def _(h):
        s = picker(off_ref[h]).astype(jnp.bfloat16)
        g_sel[h] = mm(s, g_ref[:, head_cols(h)]).astype(jnp.bfloat16)

    to_group(g_sel, g_all, 3)
    lse_cols[...] = jnp.zeros_like(lse_cols)

    @pl.loop(0, HEADS)
    def _(h):
        v1 = with_ones(v_ref[:, head_cols(h)])
        k = k_ref[:, head_cols(h)]
        for r in range(2):
            rows = slice(r * 256, r * 256 + 256)
            o, lse = softmax_out(q_ref[rows, head_cols(h)], k, v1)
            near_out[rows, head_cols(h)] = o.astype(jnp.bfloat16)
            lane = lax.broadcasted_iota(jnp.int32, (256, 128), 1)
            lse_cols[rows] = jnp.where(lane == h, lse, lse_cols[rows])

    wait_bytes(q_all.at[pl.ds(0, 7)], recv_sem.at[1])
    wait_bytes(kv_all.at[:, pl.ds(0, 63)], recv_sem.at[0])
    q = q_all[...].reshape(256, DIM)
    k = kv_all[0].reshape(2048, DIM)
    v1 = with_ones(kv_all[1].reshape(2048, DIM))
    far = [softmax_out(q[r * 128:r * 128 + 128], k, v1) for r in range(2)]
    far_out = jnp.concatenate([f[0] for f in far], axis=0)
    far_lse = jnp.concatenate([f[1] for f in far], axis=0)
    wait_bytes(os_all.at[pl.ds(0, 7)], recv_sem.at[2])
    near_sel = os_all[:, 0].reshape(256, DIM)
    near_lse = os_all[:, 1].reshape(256, DIM)
    top = jnp.maximum(near_lse, far_lse)
    mixed = top + jnp.log(jnp.exp2(near_lse - top) + jnp.exp2(far_lse - top)) * LOG2E
    att = (jnp.exp2(near_lse - mixed) * near_sel + jnp.exp2(far_lse - mixed) * far_out).astype(jnp.bfloat16)
    back_att[...] = att.reshape(HOLD, PICK, DIM)
    wait_bytes(g_all.at[pl.ds(0, 7)], recv_sem.at[3])
    g = g_all[...].reshape(256, DIM)
    delta = jnp.sum(g.astype(jnp.float32) * att.astype(jnp.float32), axis=1, keepdims=True)
    lane = lax.broadcasted_iota(jnp.int32, (256, DIM), 1)
    stat = jnp.where(lane < 64, mixed, delta)
    back_stat[...] = stat.reshape(HOLD, PICK, DIM)
    to_group(back_att, got_att, 4)
    to_group(back_stat, got_stat, 5)
    stat_t = stat.T
    mixed_lane = stat_t[0:1, :]
    delta_lane = stat_t[64:65, :]
    dq_acc[...] = jnp.zeros_like(dq_acc)

    @pl.loop(0, 4)
    def _(c):
        blocks = pl.ds(c * 16, 16)
        kc = kv_all[0, blocks].reshape(512, DIM)
        vc = kv_all[1, blocks].reshape(512, DIM)
        qq = q_all[...].reshape(256, DIM)
        gg = g_all[...].reshape(256, DIM)
        p = jnp.exp2(mm(kc, qq, NT) * SCALE2 - mixed_lane)
        ds = (p * (mm(vc, gg, NT) - delta_lane)).astype(jnp.bfloat16)
        dkv_ref[0, blocks] = (mm(ds, qq) * SCALE).astype(jnp.bfloat16).reshape(16, PICK, DIM)
        dkv_ref[1, blocks] = mm(p.astype(jnp.bfloat16), gg).astype(jnp.bfloat16).reshape(16, PICK, DIM)
        dq_acc[...] += mm(ds, kc, TN)

    dq_ref[...] = (dq_acc[...] * SCALE).astype(jnp.bfloat16).reshape(HOLD, PICK, DIM)

    lse_t = lse_cols[...].T
    lse_ref[...] = lse_t[0:HEADS, :]
    wait_bytes(got_att.at[pl.ds(0, 7)], recv_sem.at[4])
    wait_bytes(got_stat.at[pl.ds(0, 7)], recv_sem.at[5])

    for h in range(HEADS):
        pick = picker(off_ref[h])
        st = got_stat[h]
        mixed_h = jnp.sum(jnp.where(pick, st[:, 0:1], 0.0), axis=0, keepdims=True)
        delta_h = jnp.sum(jnp.where(pick, st[:, 64:65], 0.0), axis=0, keepdims=True)
        lane1 = lax.rem(lax.broadcasted_iota(jnp.int32, (1, TOK), 1), RATE)
        lse_ref[h:h + 1, :] = jnp.where(lane1 == off_ref[h], mixed_h, lse_ref[h:h + 1, :])
        delta_ref[h:h + 1, :] = delta_h
        cols = slice(h * DIM, h * DIM + DIM)
        put = mm(pick.astype(jnp.bfloat16), got_att[h], TN)
        rowmod = lax.rem(lax.broadcasted_iota(jnp.int32, (TOK, DIM), 0), RATE)
        att_ref[:, cols] = jnp.where(rowmod == off_ref[h], put, near_out[:, cols].astype(jnp.float32)).astype(jnp.bfloat16)

    wait_bytes(kv_all.at[:, pl.ds(0, 63)], send_sem.at[0])
    wait_bytes(q_all.at[pl.ds(0, 7)], send_sem.at[1])
    wait_bytes(os_all.at[pl.ds(0, 7)], send_sem.at[2])
    wait_bytes(g_all.at[pl.ds(0, 7)], send_sem.at[3])
    wait_bytes(got_att.at[pl.ds(0, 7)], send_sem.at[4])
    wait_bytes(got_stat.at[pl.ds(0, 7)], send_sem.at[5])


def far_call(offsets, q, k, v, w, grad):
    bf, f32 = jnp.bfloat16, jnp.float32
    vm = pl.BlockSpec(memory_space=pltpu.VMEM)
    S = jax.ShapeDtypeStruct
    return pl.pallas_call(
        far_kernel,
        out_shape=(S((TOK, 1024), bf), S((TOK, 1024), bf), S((HEADS, TOK), f32), S((HEADS, TOK), f32),
                   S((2, 64, PICK, DIM), bf), S((HOLD, PICK, DIM), bf)),
        in_specs=[pl.BlockSpec(memory_space=pltpu.SMEM), vm, vm, vm, pl.BlockSpec(memory_space=pl.ANY), pl.BlockSpec(memory_space=pl.ANY)],
        out_specs=(vm,) * 6,
        scratch_shapes=[
            pltpu.VMEM((1024, 2048), bf), pltpu.VMEM((TOK, 2048), bf),
            pltpu.VMEM((HEADS, 2, PICK, DIM), bf), pltpu.VMEM((HEADS, PICK, DIM), bf), pltpu.VMEM((HEADS, PICK, DIM), bf),
            pltpu.VMEM((HEADS, 2, PICK, DIM), f32),
            pltpu.VMEM((2, 64, PICK, DIM), bf), pltpu.VMEM((HOLD, PICK, DIM), bf), pltpu.VMEM((HOLD, PICK, DIM), bf),
            pltpu.VMEM((HOLD, 2, PICK, DIM), f32),
            pltpu.VMEM((HOLD, PICK, DIM), bf), pltpu.VMEM((HOLD, PICK, DIM), f32),
            pltpu.VMEM((HOLD, PICK, DIM), bf), pltpu.VMEM((HOLD, PICK, DIM), f32),
            pltpu.VMEM((TOK, 1024), bf), pltpu.VMEM((TOK, 128), f32), pltpu.VMEM((256, DIM), f32),
            pltpu.SemaphoreType.DMA((2,)), pltpu.SemaphoreType.DMA((6,)), pltpu.SemaphoreType.DMA((6,)),
        ],
        compiler_params=pltpu.CompilerParams(collective_id=1, has_side_effects=True, vmem_limit_bytes=60 * 1024 * 1024),
    )(offsets, q, k, v, w, grad)


STRIDES = (16, 4, 1)
ORDERS = ((0, 1, 2), (1, 2, 0), (2, 0, 1))
WIDTHS = (384, 384, 384, 384, 256, 256)
STARTS = (0, 384, 768, 1152, 1536, 1792)
PARTS = [(ORDERS[p % 3], p // 3) for p in range(6)]
STEP_ROWS = (256, 128, 64, 32)
STEP_OFF = (0, 256, 384, 448)


def sum_kernel(off_ref, att_ref, grad_ref, lse_ref, delta_ref, q_hbm, k_hbm, v_hbm, g_hbm, w_hbm, dkv_hbm, dqf_hbm,
               res_hbm, dq_hbm, dk_hbm, dv_hbm, out_ref,
               q_ref, k_ref, v_ref, g_ref, w_ref, res_ref, dq_ref, dk_ref, dv_ref, got_dkv, got_dq,
               flat_t, acc, s0, r0, sbuf, rbuf, last, load_sem, store_sem, far_sem, send_sem, recv_sem):
    dp = lax.axis_index("dp")
    seq = lax.axis_index("seq")
    my_head, my_part = seq // HOLD, seq % HOLD
    coord = [(seq // st) % 4 for st in STRIDES]
    barrier = pltpu.get_barrier_semaphore()
    sibling = (1 - dp, seq)
    pl.semaphore_signal(barrier, inc=1, device_id=sibling, device_id_type=MESH)

    @pl.loop(1, 64)
    def _(i):
        pl.semaphore_signal(barrier, inc=1, device_id=(dp, lax.rem(seq + i, 64)), device_id_type=MESH)

    loads = [pltpu.make_async_copy(s, d, load_sem.at[i]) for i, (s, d) in enumerate(
        ((q_hbm, q_ref), (k_hbm, k_ref), (v_hbm, v_ref), (g_hbm, g_ref), (w_hbm, w_ref)))]
    for load in loads:
        load.start()

    def peer(axis, c):
        return (dp, seq + (c - coord[axis]) * STRIDES[axis])

    flat_t[...] = att_ref[...].T
    mine = pl.multiple_of(dp * 512, 512)
    other = pl.multiple_of((1 - dp) * 512, 512)

    def copy(p, k, src, dst, target):
        return pltpu.make_async_remote_copy(src_ref=src, dst_ref=dst, send_sem=send_sem.at[p, k], recv_sem=recv_sem.at[p, k], device_id=target, device_id_type=MESH)

    cols = [slice(STARTS[p], STARTS[p] + WIDTHS[p]) for p in range(6)]
    started = []
    stores = []
    first = []
    for p in range(6):
        s0[:, cols[p]] = mm(flat_t[pl.ds(other, 512), :], grad_ref[:, cols[p]]).astype(jnp.bfloat16)
        if p == 0:
            pl.semaphore_wait(barrier, 64)
        c = copy(p, 0, s0.at[:, cols[p]], r0.at[:, cols[p]], sibling)
        c.start()
        first.append(c)
    started += first

    own = [pltpu.make_async_copy(dkv_hbm.at[:, seq], got_dkv.at[seq], load_sem.at[5]),
           pltpu.make_async_copy(dqf_hbm.at[my_head], got_dq.at[my_head], load_sem.at[6])]
    for c in own:
        c.start()

    @pl.loop(1, 64)
    def _(i):
        d = lax.rem(seq + i, 64)
        pltpu.make_async_remote_copy(
            src_ref=dkv_hbm.at[:, d], dst_ref=got_dkv.at[seq], send_sem=far_sem.at[0], recv_sem=far_sem.at[1],
            device_id=(dp, d), device_id_type=MESH).start()

    @pl.loop(1, HEADS)
    def _(i):
        h = lax.rem(my_head + i, HEADS)
        pltpu.make_async_remote_copy(
            src_ref=dqf_hbm.at[h], dst_ref=got_dq.at[my_head], send_sem=far_sem.at[2], recv_sem=far_sem.at[3],
            device_id=(dp, h * HOLD + my_part), device_id_type=MESH).start()

    for p in range(6):
        acc[:, cols[p]] = mm(flat_t[pl.ds(mine, 512), :], grad_ref[:, cols[p]])

    def project(c):
        if c == 0:
            loads[4].wait()
        cs = slice(c * 512, c * 512 + 512)
        res_ref[:, cs] = mm(att_ref[...], w_ref[:, cs]).astype(jnp.bfloat16)
        st = pltpu.make_async_copy(res_ref.at[:, cs], res_hbm.at[:, cs], store_sem.at[0, c])
        st.start()
        stores.append(st)

    def returned():
        for load in loads[:4] + own:
            load.wait()
        wait_bytes(got_dkv.at[pl.ds(0, 63)], far_sem.at[1])
        wait_bytes(got_dq.at[pl.ds(0, 7)], far_sem.at[3])

    def near_back(h):
        hs = slice(h * DIM, h * DIM + DIM)
        off = off_ref[h]
        q, k, g = q_ref[:, hs], k_ref[:, hs], g_ref[:, hs]
        probs = jnp.exp2(mm(k, q, NT) * SCALE2 - lse_ref[h:h + 1, :])
        low = probs.astype(jnp.bfloat16)
        prod = probs * mm(v_ref[:, hs], g, NT)
        lane = lax.rem(lax.broadcasted_iota(jnp.int32, (1, TOK), 1), RATE)
        delta = jnp.where(lane == off, delta_ref[h:h + 1, :], jnp.sum(prod, axis=0, keepdims=True))
        ds = (prod - probs * delta).astype(jnp.bfloat16)
        put = (lax.broadcasted_iota(jnp.int32, (TOK, HOLD * PICK), 0)
               == lax.rem(lax.broadcasted_iota(jnp.int32, (TOK, HOLD * PICK), 1), PICK) * RATE + off).astype(jnp.bfloat16)
        far = slice(h * HOLD, h * HOLD + HOLD)
        dv_ref[:, hs] = (mm(low, g) + mm(put, got_dkv[far, 1].reshape(HOLD * PICK, DIM))).astype(jnp.bfloat16)
        dk_ref[:, hs] = (mm(ds, q) * SCALE + mm(put, got_dkv[far, 0].reshape(HOLD * PICK, DIM))).astype(jnp.bfloat16)
        dq_ref[:, hs] = (mm(ds, k, TN) * SCALE + mm(put[:, :PICK], got_dq[h])).astype(jnp.bfloat16)
        for i, (a, b) in enumerate(((dq_ref, dq_hbm), (dk_ref, dk_hbm), (dv_ref, dv_hbm))):
            st = pltpu.make_async_copy(a.at[:, hs], b.at[:, hs], store_sem.at[1 + i, h])
            st.start()
            stores.append(st)

    base = [0] * 6
    flight = [None] * 6
    history = [[] for _ in range(6)]

    def launch(p, s):
        order, swap = PARTS[p]
        axis = order[s // 2]
        c = coord[axis]
        if (s % 2) == swap:
            bit, target = ((c + 1) // 2) % 2, peer(axis, c + 1 - 2 * (c % 2))
        else:
            bit, target = c // 2, peer(axis, 3 - c)
        n = STEP_ROWS[s]
        keep = pl.multiple_of(base[p] + bit * n, n)
        send = pl.multiple_of(base[p] + (1 - bit) * n, n)
        rows = slice(STEP_OFF[s], STEP_OFF[s] + n)
        sbuf[rows, cols[p]] = acc[pl.ds(send, n), cols[p]].astype(jnp.bfloat16)
        cp = copy(p, 1 + s, sbuf.at[rows, cols[p]], rbuf.at[rows, cols[p]], target)
        cp.start()
        started.append(cp)
        history[p].append((keep, send, target))
        base[p] = keep
        flight[p] = cp

    for p in range(6):
        first[p].wait_recv()
        acc[:, cols[p]] += r0[:, cols[p]].astype(jnp.float32)
        launch(p, 0)
    for c in range(4):
        project(c)
    lasts = [None] * 6
    for s in range(4):
        n = STEP_ROWS[s]
        rows = slice(STEP_OFF[s], STEP_OFF[s] + n)
        for p in range(6):
            flight[p].wait_recv()
            acc[pl.ds(base[p], n), cols[p]] += rbuf[rows, cols[p]].astype(jnp.float32)
            if s < 3:
                launch(p, s + 1)
            else:
                axis = PARTS[p][0][2]
                sbuf[480:512, cols[p]] = acc[pl.ds(base[p], 32), cols[p]].astype(jnp.bfloat16)
                lasts[p] = []
                for d in (1, 2, 3):
                    cp = copy(p, 4 + d, sbuf.at[480:512, cols[p]], last.at[d - 1, :, cols[p]], peer(axis, (coord[axis] + d) % 4))
                    cp.start()
                    started.append(cp)
                    lasts[p].append(cp)
        if s == 0:
            returned()
        near_back(s)
    gather = [None] * 6
    for p in range(6):
        for d in (1, 2, 3):
            lasts[p][d - 1].wait_recv()
        total = sbuf[480:512, cols[p]].astype(jnp.float32)
        for d in (1, 2, 3):
            total = total + last[d - 1, :, cols[p]].astype(jnp.float32)
        rows = pl.ds(pl.multiple_of(mine + base[p], 32), 32)
        out_ref[rows, cols[p]] = total.astype(jnp.bfloat16)
        here = out_ref.at[rows, cols[p]]
        cp = copy(p, 8, here, here, history[p][3][2])
        cp.start()
        started.append(cp)
        gather[p] = cp
    near_back(4)
    final = []
    for s in (3, 2, 1, 0):
        for p in range(6):
            gather[p].wait_recv()
            n = STEP_ROWS[s]
            if s > 0:
                start = pl.multiple_of(mine + history[p][s - 1][0], 2 * n)
                here = out_ref.at[pl.ds(start, 2 * n), cols[p]]
                cp = copy(p, 12 - s, here, here, history[p][s - 1][2])
                cp.start()
                started.append(cp)
                gather[p] = cp
                if s == 1:
                    final.append(copy(p, 12, here, here, sibling))
                    final[-1].start()
            else:
                start = pl.multiple_of(mine + history[p][0][1], n)
                here = out_ref.at[pl.ds(start, n), cols[p]]
                final.append(copy(p, 13, here, here, sibling))
                final[-1].start()
        if s > 0:
            near_back(8 - s)
    for cp in final:
        cp.wait_recv()
    for cp in started + final:
        cp.wait_send()
    for st in stores:
        st.wait()
    wait_bytes(got_dkv.at[pl.ds(0, 63)], far_sem.at[0])
    wait_bytes(got_dq.at[pl.ds(0, 7)], far_sem.at[2])


def sum_call(offsets, att, grad, lse, delta, q, k, v, g, w, dkv, dqf):
    bf, f32 = jnp.bfloat16, jnp.float32
    vm = pl.BlockSpec(memory_space=pltpu.VMEM)
    anyspace = pl.BlockSpec(memory_space=pl.ANY)
    S = jax.ShapeDtypeStruct
    V = pltpu.VMEM
    return pl.pallas_call(
        sum_kernel,
        out_shape=(S((TOK, 2048), bf), S((TOK, 1024), bf), S((TOK, 1024), bf), S((TOK, 1024), bf), S((1024, 2048), bf)),
        in_specs=[pl.BlockSpec(memory_space=pltpu.SMEM)] + [vm] * 4 + [anyspace] * 7,
        out_specs=(anyspace,) * 4 + (vm,),
        scratch_shapes=[
            V((TOK, 1024), bf), V((TOK, 1024), bf), V((TOK, 1024), bf), V((TOK, 1024), bf), V((1024, 2048), bf),
            V((TOK, 2048), bf), V((TOK, 1024), bf), V((TOK, 1024), bf), V((TOK, 1024), bf),
            V((64, 2, PICK, DIM), bf), V((HEADS, PICK, DIM), bf),
            V((1024, 512), bf), V((512, 2048), f32), V((512, 2048), bf), V((512, 2048), bf), V((512, 2048), bf),
            V((512, 2048), bf), V((3, 32, 2048), bf),
            pltpu.SemaphoreType.DMA((7,)), pltpu.SemaphoreType.DMA((4, 8)), pltpu.SemaphoreType.DMA((4,)),
            pltpu.SemaphoreType.DMA((6, 14)), pltpu.SemaphoreType.DMA((6, 14)),
        ],
        compiler_params=pltpu.CompilerParams(collective_id=0, has_side_effects=True, vmem_limit_bytes=60 * 1024 * 1024),
    )(offsets, att, grad, lse, delta, q, k, v, g, w, dkv, dqf)


def per_device(queries, keys, values, offsets, out_weight, grad_out):
    q, k, v, grad = queries[0], keys[0], values[0], grad_out[0]
    att, g, lse, delta, dkv, dqf = far_call(offsets, q, k, v, out_weight, grad)
    res, dq, dk, dv, total = sum_call(offsets, att, grad, lse, delta, q, k, v, g, out_weight, dkv, dqf)
    weight_grad = total.astype(jnp.float32) * (1.0 / math.sqrt(65536))
    return res[None], dq[None], dk[None], dv[None], weight_grad


def solution(mesh):
    split = P("dp", "seq", None)
    return jax.shard_map(
        per_device, mesh=mesh, in_specs=(split, split, split, P(), P(), split),
        out_specs=(split, split, split, split, P()), check_vma=False)
```

```python
import math

import jax
import jax.numpy as jnp
from jax import lax
from jax.experimental import pallas as pl
from jax.experimental.pallas import tpu as pltpu
from jax.sharding import PartitionSpec as P

MESH = pl.DeviceIdType.MESH

RATE = 16
HEADS = 8
DIM = 128
TOK = 512
PICK = 32
HOLD = 8
SCALE = DIM ** -0.5
LOG2E = math.log2(math.e)
SCALE2 = SCALE * LOG2E
NT = (((1,), (1,)), ((), ()))
TN = (((0,), (0,)), ((), ()))


def mm(a, b, dims=(((1,), (0,)), ((), ()))):
    return lax.dot_general(a, b, dims, preferred_element_type=jnp.float32)


def head_cols(h):
    return pl.ds(pl.multiple_of(h * DIM, DIM), DIM)


def picker(off):
    row = lax.broadcasted_iota(jnp.int32, (PICK, TOK), 0)
    pos = lax.broadcasted_iota(jnp.int32, (PICK, TOK), 1)
    return pos == row * RATE + off


def with_ones(value):
    return jnp.concatenate([value, jnp.ones_like(value)], axis=1)


def softmax_out(q, k, v1):
    s = mm(q, k, NT)
    top = jnp.max(s, axis=1, keepdims=True) * SCALE2
    e = jnp.exp2(s * SCALE2 - top).astype(jnp.bfloat16)
    ov = mm(e, v1)
    total = ov[:, DIM:]
    return ov[:, :DIM] / total, top + jnp.log(total) * LOG2E


def wait_bytes(ref, sem):
    pltpu.make_async_copy(ref, ref, sem).wait()


STRIDES = (16, 4, 1)
WIDTHS = (384, 384, 384, 384, 256, 256)
STARTS = (0, 384, 768, 1152, 1536, 1792)
COLS = [slice(a, a + b) for a, b in zip(STARTS, WIDTHS)]
ORDERS = ((0, 1, 2), (1, 2, 0), (2, 0, 1)) * 2


def layer_kernel(off_ref, q_hbm, k_hbm, v_hbm, w_hbm, grad_hbm,
                 res_hbm, dq_hbm, dk_hbm, dv_hbm, total_hbm,
                 q_ref, k_ref, v_ref, w_ref, grad_ref, g_ref, att_ref, res_ref, dq_ref, dk_ref, dv_ref,
                 kv_sel, q_sel, g_sel, os_sel, kv_all, q_all, g_all, os_all,
                 back_att, back_stat, got_att, got_stat, dkv, dqf, got_dkv, got_dq,
                 near_t, lse_cols, lse_ref, delta_ref, dq_acc, dqn_acc, dk_acc, dv_acc,
                 acc, s0, r0, sbuf, rbuf1, rbuf2, last, total_ref,
                 load_sem, store_sem, far_send, far_recv, send_sem, recv_sem):
    dp = lax.axis_index("dp")
    seq = lax.axis_index("seq")
    my_head, my_part = seq // HOLD, seq % HOLD
    coord = [(seq // st) % 4 for st in STRIDES]
    sibling = (1 - dp, seq)
    barrier = pltpu.get_barrier_semaphore()
    loads = [pltpu.make_async_copy(s, d, load_sem.at[i]) for i, (s, d) in enumerate(
        ((k_hbm, k_ref), (v_hbm, v_ref), (q_hbm, q_ref), (w_hbm, w_ref), (grad_hbm, grad_ref)))]
    for load in loads:
        load.start()
    pl.semaphore_signal(barrier, inc=1, device_id=sibling, device_id_type=MESH)

    @pl.loop(1, 64)
    def _(i):
        pl.semaphore_signal(barrier, inc=1, device_id=(dp, lax.rem(seq + i, 64)), device_id_type=MESH)

    started = []
    stores = []

    def store(src, dst, sem):
        st = pltpu.make_async_copy(src, dst, sem)
        st.start()
        stores.append(st)

    def to_group(src, dst, k):
        @pl.loop(1, HEADS)
        def _(i):
            h = lax.rem(my_head + i, HEADS)
            pltpu.make_async_remote_copy(
                src_ref=src.at[h], dst_ref=dst.at[my_head], send_sem=far_send.at[k], recv_sem=far_recv.at[k],
                device_id=(dp, h * HOLD + my_part), device_id_type=MESH).start()
        dst[my_head] = src[my_head]

    loads[0].wait()
    loads[1].wait()

    @pl.loop(0, HEADS)
    def _(h):
        s = picker(off_ref[h]).astype(jnp.bfloat16)
        kv_sel[h, 0] = mm(s, k_ref[:, head_cols(h)]).astype(jnp.bfloat16)
        kv_sel[h, 1] = mm(s, v_ref[:, head_cols(h)]).astype(jnp.bfloat16)

    pl.semaphore_wait(barrier, 64)

    @pl.loop(1, 64)
    def _(i):
        d = lax.rem(seq + i, 64)
        pltpu.make_async_remote_copy(
            src_ref=kv_sel.at[d // HOLD], dst_ref=kv_all.at[:, seq], send_sem=far_send.at[0], recv_sem=far_recv.at[0],
            device_id=(dp, d), device_id_type=MESH).start()

    kv_all[:, seq] = kv_sel[my_head]

    loads[2].wait()

    @pl.loop(0, HEADS)
    def _(h):
        s = picker(off_ref[h]).astype(jnp.bfloat16)
        q_sel[h] = mm(s, q_ref[:, head_cols(h)]).astype(jnp.bfloat16)

    to_group(q_sel, q_all, 1)

    @pl.loop(0, HEADS)
    def _(h):
        o, lse = softmax_out(q_sel[h], k_ref[:, head_cols(h)], with_ones(v_ref[:, head_cols(h)]))
        os_sel[h, 0] = o
        os_sel[h, 1] = lse

    to_group(os_sel, os_all, 2)

    loads[3].wait()
    loads[4].wait()

    @pl.loop(0, 4)
    def _(c):
        cols = pl.ds(pl.multiple_of(c * 256, 256), 256)
        g_ref[:, cols] = mm(grad_ref[...], w_ref[cols, :], NT).astype(jnp.bfloat16)

    @pl.loop(0, HEADS)
    def _(h):
        s = picker(off_ref[h]).astype(jnp.bfloat16)
        g_sel[h] = mm(s, g_ref[:, head_cols(h)]).astype(jnp.bfloat16)

    to_group(g_sel, g_all, 3)

    lse_cols[...] = jnp.zeros_like(lse_cols)

    @pl.loop(0, HEADS)
    def _(h):
        v1 = with_ones(v_ref[:, head_cols(h)])
        k = k_ref[:, head_cols(h)]
        for r in range(2):
            rows = slice(r * 256, r * 256 + 256)
            o, lse = softmax_out(q_ref[rows, head_cols(h)], k, v1)
            near_t[head_cols(h), rows] = o.astype(jnp.bfloat16).T
            lane = lax.broadcasted_iota(jnp.int32, (256, 128), 1)
            lse_cols[rows] = jnp.where(lane == h, lse, lse_cols[rows])

    wait_bytes(q_all.at[pl.ds(0, 7)], far_recv.at[1])
    wait_bytes(kv_all.at[:, pl.ds(0, 63)], far_recv.at[0])
    q = q_all[...].reshape(256, DIM)
    k = kv_all[0].reshape(2048, DIM)
    v1 = with_ones(kv_all[1].reshape(2048, DIM))
    far = [softmax_out(q[r * 128:r * 128 + 128], k, v1) for r in range(2)]
    far_out = jnp.concatenate([f[0] for f in far], axis=0)
    far_lse = jnp.concatenate([f[1] for f in far], axis=0)
    wait_bytes(os_all.at[pl.ds(0, 7)], far_recv.at[2])
    near_sel = os_all[:, 0].reshape(256, DIM)
    near_lse = os_all[:, 1].reshape(256, DIM)
    top = jnp.maximum(near_lse, far_lse)
    mixed = top + jnp.log(jnp.exp2(near_lse - top) + jnp.exp2(far_lse - top)) * LOG2E
    att = (jnp.exp2(near_lse - mixed) * near_sel + jnp.exp2(far_lse - mixed) * far_out).astype(jnp.bfloat16)
    back_att[...] = att.reshape(HOLD, PICK, DIM)
    to_group(back_att, got_att, 4)
    wait_bytes(g_all.at[pl.ds(0, 7)], far_recv.at[3])
    g = g_all[...].reshape(256, DIM)
    delta = jnp.sum(g.astype(jnp.float32) * att.astype(jnp.float32), axis=1, keepdims=True)
    lane = lax.broadcasted_iota(jnp.int32, (256, DIM), 1)
    stat = jnp.where(lane < 64, mixed, delta)
    back_stat[...] = stat.reshape(HOLD, PICK, DIM)
    to_group(back_stat, got_stat, 5)
    stat_t = stat.T
    mixed_lane = stat_t[0:1, :]
    delta_lane = stat_t[64:65, :]
    dq_acc[...] = jnp.zeros_like(dq_acc)

    @pl.loop(0, 4)
    def _(c):
        blocks = pl.ds(c * 16, 16)
        kc = kv_all[0, blocks].reshape(512, DIM)
        vc = kv_all[1, blocks].reshape(512, DIM)
        qq = q_all[...].reshape(256, DIM)
        gg = g_all[...].reshape(256, DIM)
        p = jnp.exp2(mm(kc, qq, NT) * SCALE2 - mixed_lane)
        ds = (p * (mm(vc, gg, NT) - delta_lane)).astype(jnp.bfloat16)
        dkv[0, blocks] = (mm(ds, qq) * SCALE).astype(jnp.bfloat16).reshape(16, PICK, DIM)
        dkv[1, blocks] = mm(p.astype(jnp.bfloat16), gg).astype(jnp.bfloat16).reshape(16, PICK, DIM)
        dq_acc[...] += mm(ds, kc, TN)

    dqf[...] = (dq_acc[...] * SCALE).astype(jnp.bfloat16).reshape(HOLD, PICK, DIM)

    @pl.loop(1, 64)
    def _(i):
        d = lax.rem(seq + i, 64)
        pltpu.make_async_remote_copy(
            src_ref=dkv.at[:, d], dst_ref=got_dkv.at[seq], send_sem=far_send.at[6], recv_sem=far_recv.at[6],
            device_id=(dp, d), device_id_type=MESH).start()

    got_dkv[seq] = dkv[:, seq]
    to_group(dqf, got_dq, 7)

    wait_bytes(got_att.at[pl.ds(0, 7)], far_recv.at[4])
    lane1 = lax.rem(lax.broadcasted_iota(jnp.int32, (1, TOK), 1), RATE)
    for h in range(HEADS):
        rows = slice(h * DIM, h * DIM + DIM)
        put = mm(got_att[h], picker(off_ref[h]).astype(jnp.bfloat16), TN)
        near_t[rows, :] = jnp.where(lane1 == off_ref[h], put, near_t[rows, :].astype(jnp.float32)).astype(jnp.bfloat16)

    def peer(axis, d):
        c = lax.rem(coord[axis] + d, 4)
        return c, (dp, seq + (c - coord[axis]) * STRIDES[axis])

    def copy(p, k, src, dst, target):
        cp = pltpu.make_async_remote_copy(
            src_ref=src, dst_ref=dst, send_sem=send_sem.at[p, k], recv_sem=recv_sem.at[p, k],
            device_id=target, device_id_type=MESH)
        cp.start()
        started.append(cp)
        return cp

    mine = pl.multiple_of(dp * 512, 512)
    other = pl.multiple_of((1 - dp) * 512, 512)
    first = []
    for p in range(6):
        s0[:, COLS[p]] = mm(near_t[pl.ds(other, 512), :], grad_ref[:, COLS[p]]).astype(jnp.bfloat16)
        first.append(copy(p, 0, s0.at[:, COLS[p]], r0.at[:, COLS[p]], sibling))
    for p in range(6):
        acc[:, COLS[p]] = mm(near_t[pl.ds(mine, 512), :], grad_ref[:, COLS[p]])

    flight = [None] * 6

    def send_rows(p, level, base, n, buf, landing):
        axis = ORDERS[p][level]
        flight[p] = []
        for d in (1, 2, 3):
            c, target = peer(axis, d)
            rows = slice((d - 1) * n, d * n)
            buf[rows, COLS[p]] = acc[pl.ds(pl.multiple_of(base + c * n, n), n), COLS[p]].astype(jnp.bfloat16)
            flight[p].append(copy(p, 1 + 3 * level + d - 1, buf.at[rows, COLS[p]], landing.at[rows, COLS[p]], target))

    base1 = []
    for p in range(6):
        first[p].wait_recv()
        acc[:, COLS[p]] += r0[:, COLS[p]].astype(jnp.float32)
        send_rows(p, 0, 0, 128, sbuf, rbuf1)
        base1.append(pl.multiple_of(coord[ORDERS[p][0]] * 128, 128))

    def statistics():
        lse_ref[...] = lse_cols[...].T[0:HEADS, :]
        wait_bytes(got_stat.at[pl.ds(0, 7)], far_recv.at[5])
        for h in range(HEADS):
            pick = picker(off_ref[h])
            st = got_stat[h]
            mixed_h = jnp.sum(jnp.where(pick, st[:, 0:1], 0.0), axis=0, keepdims=True)
            lse_ref[h:h + 1, :] = jnp.where(lane1 == off_ref[h], mixed_h, lse_ref[h:h + 1, :])
            delta_ref[h:h + 1, :] = jnp.sum(jnp.where(pick, st[:, 64:65], 0.0), axis=0, keepdims=True)

    def project(c):
        cs = slice(c * 512, c * 512 + 512)
        res_ref[:, cs] = mm(att_ref[...], w_ref[:, cs]).astype(jnp.bfloat16)
        store(res_ref.at[:, cs], res_hbm.at[:, cs], store_sem.at[0, c])

    def returned():
        wait_bytes(got_dkv.at[pl.ds(0, 63)], far_recv.at[6])
        wait_bytes(got_dq.at[pl.ds(0, 7)], far_recv.at[7])

    def near_back(h):
        hs = slice(h * DIM, h * DIM + DIM)
        off = off_ref[h]
        q, k, g = q_ref[:, hs], k_ref[:, hs], g_ref[:, hs]
        probs = jnp.exp2(mm(k, q, NT) * SCALE2 - lse_ref[h:h + 1, :])
        low = probs.astype(jnp.bfloat16)
        prod = probs * mm(v_ref[:, hs], g, NT)
        delta = jnp.where(lane1 == off, delta_ref[h:h + 1, :], jnp.sum(prod, axis=0, keepdims=True))
        ds = (prod - probs * delta).astype(jnp.bfloat16)
        dv_acc[:, hs] = mm(low, g)
        dk_acc[:, hs] = mm(ds, q) * SCALE
        dqn_acc[:, hs] = mm(ds, k, TN) * SCALE

    def deposit(h):
        hs = slice(h * DIM, h * DIM + DIM)
        off = off_ref[h]
        put = (lax.broadcasted_iota(jnp.int32, (TOK, HOLD * PICK), 0)
               == lax.rem(lax.broadcasted_iota(jnp.int32, (TOK, HOLD * PICK), 1), PICK) * RATE + off).astype(jnp.bfloat16)
        far = slice(h * HOLD, h * HOLD + HOLD)
        dv_ref[:, hs] = (dv_acc[:, hs] + mm(put, got_dkv[far, 1].reshape(HOLD * PICK, DIM))).astype(jnp.bfloat16)
        dk_ref[:, hs] = (dk_acc[:, hs] + mm(put, got_dkv[far, 0].reshape(HOLD * PICK, DIM))).astype(jnp.bfloat16)
        dq_ref[:, hs] = (dqn_acc[:, hs] + mm(put[:, :PICK], got_dq[h])).astype(jnp.bfloat16)
        for i, (a, b) in enumerate(((dq_ref, dq_hbm), (dk_ref, dk_hbm), (dv_ref, dv_hbm))):
            store(a.at[:, hs], b.at[:, hs], store_sem.at[1 + i, h])

    att_ref[...] = near_t[...].T
    for c in range(4):
        project(c)
    statistics()
    near_back(0)
    near_back(1)
    near_back(2)

    def add_received(p, base, n, landing):
        for cp in flight[p]:
            cp.wait_recv()
        rows = pl.ds(pl.multiple_of(base, n), n)
        total = acc[rows, COLS[p]]
        for d in range(3):
            total += landing[d * n:d * n + n, COLS[p]].astype(jnp.float32)
        acc[rows, COLS[p]] = total

    base2 = []
    for p in range(6):
        add_received(p, base1[p], 128, rbuf1)
        send_rows(p, 1, base1[p], 32, sbuf.at[384:480], rbuf2)
        base2.append(pl.multiple_of(base1[p] + coord[ORDERS[p][1]] * 32, 32))
    near_back(3)
    near_back(4)
    for p in range(6):
        add_received(p, base2[p], 32, rbuf2)
        axis = ORDERS[p][2]
        here = coord[axis]
        last[here, :, COLS[p]] = acc[pl.ds(base2[p], 32), COLS[p]].astype(jnp.bfloat16)
        flight[p] = []
        for d in (1, 2, 3):
            _, target = peer(axis, d)
            flight[p].append(copy(p, 6 + d, last.at[here, :, COLS[p]], last.at[here, :, COLS[p]], target))
    near_back(5)
    near_back(6)
    for p in range(6):
        for cp in flight[p]:
            cp.wait_recv()
        total = last[0, :, COLS[p]].astype(jnp.float32)
        for j in (1, 2, 3):
            total += last[j, :, COLS[p]].astype(jnp.float32)
        rows = pl.ds(pl.multiple_of(mine + base2[p], 32), 32)
        total_ref[rows, COLS[p]] = total.astype(jnp.bfloat16)
        block = total_ref.at[rows, COLS[p]]
        flight[p] = [copy(p, 9 + d, block, block, peer(ORDERS[p][1], d)[1]) for d in (1, 2, 3)]
    near_back(7)
    final = []
    for p in range(6):
        for cp in flight[p]:
            cp.wait_recv()
        block = total_ref.at[pl.ds(pl.multiple_of(mine + base1[p], 128), 128), COLS[p]]
        flight[p] = [copy(p, 12 + d, block, block, peer(ORDERS[p][0], d)[1]) for d in (1, 2, 3)]
        final.append(copy(p, 16, block, block, sibling))
    returned()
    for h in range(HEADS):
        deposit(h)
    for p in range(6):
        for d in (1, 2, 3):
            flight[p][d - 1].wait_recv()
            c = lax.rem(coord[ORDERS[p][0]] + 4 - d, 4)
            block = total_ref.at[pl.ds(pl.multiple_of(mine + c * 128, 128), 128), COLS[p]]
            final.append(copy(p, 16 + d, block, block, sibling))
    mine_out = pltpu.make_async_copy(total_ref.at[pl.ds(mine, 512)], total_hbm.at[pl.ds(mine, 512)], load_sem.at[5])
    mine_out.start()
    for cp in final:
        cp.wait_recv()
    other_out = pltpu.make_async_copy(total_ref.at[pl.ds(other, 512)], total_hbm.at[pl.ds(other, 512)], load_sem.at[6])
    other_out.start()
    for cp in started:
        cp.wait_send()
    for st in stores:
        st.wait()
    wait_bytes(kv_all.at[:, pl.ds(0, 63)], far_send.at[0])
    for i, ref in ((1, q_all), (2, os_all), (3, g_all), (4, got_att), (5, got_stat), (7, got_dq)):
        wait_bytes(ref.at[pl.ds(0, 7)], far_send.at[i])
    wait_bytes(got_dkv.at[pl.ds(0, 63)], far_send.at[6])
    mine_out.wait()
    other_out.wait()


def layer_call(offsets, q, k, v, w, grad):
    bf, f32 = jnp.bfloat16, jnp.float32
    hbm = pl.BlockSpec(memory_space=pl.ANY)
    S = jax.ShapeDtypeStruct
    V = pltpu.VMEM
    wide, flat = (TOK, 2048), (TOK, 1024)
    rows = (HEADS, PICK, DIM)
    return pl.pallas_call(
        layer_kernel,
        out_shape=(S(wide, bf), S(flat, bf), S(flat, bf), S(flat, bf), S((1024, 2048), bf)),
        in_specs=[pl.BlockSpec(memory_space=pltpu.SMEM)] + [hbm] * 5,
        out_specs=(hbm,) * 5,
        scratch_shapes=[
            V(flat, bf), V(flat, bf), V(flat, bf), V((1024, 2048), bf), V(wide, bf), V(flat, bf), V(flat, bf),
            V(wide, bf), V(flat, bf), V(flat, bf), V(flat, bf),
            V((HEADS, 2, PICK, DIM), bf), V(rows, bf), V(rows, bf), V((HEADS, 2, PICK, DIM), f32),
            V((2, 64, PICK, DIM), bf), V(rows, bf), V(rows, bf), V((HOLD, 2, PICK, DIM), f32),
            V(rows, bf), V(rows, f32), V(rows, bf), V(rows, f32),
            V((2, 64, PICK, DIM), bf), V(rows, bf), V((64, 2, PICK, DIM), bf), V(rows, bf),
            V((1024, TOK), bf), V((TOK, 128), f32), V((HEADS, TOK), f32), V((HEADS, TOK), f32), V((256, DIM), f32),
            V(flat, f32), V(flat, f32), V(flat, f32),
            V(wide, f32), V(wide, bf), V(wide, bf), V(wide, bf), V((384, 2048), bf), V((96, 2048), bf),
            V((4, 32, 2048), bf), V((1024, 2048), bf),
            pltpu.SemaphoreType.DMA((7,)), pltpu.SemaphoreType.DMA((4, 8)),
            pltpu.SemaphoreType.DMA((8,)), pltpu.SemaphoreType.DMA((8,)),
            pltpu.SemaphoreType.DMA((6, 20)), pltpu.SemaphoreType.DMA((6, 20)),
        ],
        compiler_params=pltpu.CompilerParams(collective_id=0, has_side_effects=True, vmem_limit_bytes=60 * 1024 * 1024),
    )(offsets, q, k, v, w, grad)


def finish_kernel(scale, total_hbm, res_hbm, dq_hbm, dk_hbm, dv_hbm, wg_out, res_out, dq_out, dk_out, dv_out,
                  low, wide, res_ref, dq_ref, dk_ref, dv_ref, copy_sem, in_sem, out_sem):
    pieces = [slice(i * 128, i * 128 + 128) for i in range(8)]
    ins = [pltpu.make_async_copy(total_hbm.at[rows], low.at[rows], in_sem.at[i]) for i, rows in enumerate(pieces)]
    for cp in ins:
        cp.start()
    rest = ((res_hbm, res_ref, res_out), (dq_hbm, dq_ref, dq_out), (dk_hbm, dk_ref, dk_out), (dv_hbm, dv_ref, dv_out))
    copies = [pltpu.make_async_copy(a, b, copy_sem.at[0, i]) for i, (a, b, _) in enumerate(rest)]
    for cp in copies:
        cp.start()
    outs = []
    for i, rows in enumerate(pieces):
        ins[i].wait()
        wide[rows] = low[rows].astype(jnp.float32) * scale
        outs.append(pltpu.make_async_copy(wide.at[rows], wg_out.at[rows], out_sem.at[i]))
        outs[-1].start()
    for i, (_, b, c) in enumerate(rest):
        copies[i].wait()
        outs.append(pltpu.make_async_copy(b, c, copy_sem.at[1, i]))
        outs[-1].start()
    for cp in outs:
        cp.wait()


def finish_call(total, res, dq, dk, dv):
    bf = jnp.bfloat16
    hbm = pl.BlockSpec(memory_space=pl.ANY)
    S = jax.ShapeDtypeStruct
    flat = S((TOK, 1024), bf)

    def kernel(*refs):
        finish_kernel(1.0 / math.sqrt(65536), *refs)

    return pl.pallas_call(
        kernel,
        out_shape=(S((1024, 2048), jnp.float32), S((TOK, 2048), bf), flat, flat, flat),
        in_specs=[hbm] * 5,
        out_specs=(hbm,) * 5,
        scratch_shapes=[pltpu.VMEM((1024, 2048), bf), pltpu.VMEM((1024, 2048), jnp.float32),
                        pltpu.VMEM((TOK, 2048), bf), pltpu.VMEM((TOK, 1024), bf), pltpu.VMEM((TOK, 1024), bf),
                        pltpu.VMEM((TOK, 1024), bf), pltpu.SemaphoreType.DMA((2, 4)), pltpu.SemaphoreType.DMA((8,)), pltpu.SemaphoreType.DMA((8,))],
        compiler_params=pltpu.CompilerParams(vmem_limit_bytes=60 * 1024 * 1024),
    )(total, res, dq, dk, dv)


def per_device(queries, keys, values, offsets, out_weight, grad_out):
    res, dq, dk, dv, total = layer_call(offsets, queries[0], keys[0], values[0], out_weight, grad_out[0])
    weight_grad, res, dq, dk, dv = finish_call(total, res, dq, dk, dv)
    return res[None], dq[None], dk[None], dv[None], weight_grad


def solution(mesh):
    split = P("dp", "seq", None)
    return jax.shard_map(
        per_device, mesh=mesh, in_specs=(split, split, split, P(), P(), split),
        out_specs=(split, split, split, split, P()), check_vma=False)
```

```python
import math

import jax
import jax.numpy as jnp
from jax import lax
from jax.experimental import pallas as pl
from jax.experimental.pallas import tpu as pltpu
from jax.sharding import PartitionSpec as P

MESH = pl.DeviceIdType.MESH

RATE = 16
HEADS = 8
DIM = 128
TOK = 512
PICK = 32
HOLD = 8
SCALE = DIM ** -0.5
LOG2E = math.log2(math.e)
SCALE2 = SCALE * LOG2E
NT = (((1,), (1,)), ((), ()))
TN = (((0,), (0,)), ((), ()))


def mm(a, b, dims=(((1,), (0,)), ((), ()))):
    return lax.dot_general(a, b, dims, preferred_element_type=jnp.float32)


def head_cols(h):
    if isinstance(h, int):
        return slice(h * DIM, h * DIM + DIM)
    return pl.ds(pl.multiple_of(h * DIM, DIM), DIM)


def picker(off):
    row = lax.broadcasted_iota(jnp.int32, (PICK, TOK), 0)
    pos = lax.broadcasted_iota(jnp.int32, (PICK, TOK), 1)
    return pos == row * RATE + off


def with_ones(value):
    return jnp.concatenate([value, jnp.ones_like(value)], axis=1)


def softmax_out(q, k, v1):
    s = mm(q, k, NT)
    top = jnp.max(s, axis=1, keepdims=True) * SCALE2
    e = jnp.exp2(s * SCALE2 - top).astype(jnp.bfloat16)
    ov = mm(e, v1)
    total = ov[:, DIM:]
    return ov[:, :DIM] / total, top + jnp.log(total) * LOG2E


def wait_bytes(ref, sem):
    pltpu.make_async_copy(ref, ref, sem).wait()


STRIDES = (16, 4, 1)
WIDTHS = (384, 384, 384, 384, 256, 256)
STARTS = (0, 384, 768, 1152, 1536, 1792)
COLS = [slice(a, a + b) for a, b in zip(STARTS, WIDTHS)]
ORDERS = ((0, 1, 2), (1, 2, 0), (2, 0, 1)) * 2
FAR_FIRST = sorted(((a, b, c) for a in range(4) for b in range(4) for c in range(4) if a + b + c > 0),
                   key=lambda o: -sum(min(d, 4 - d) for d in o))


def layer_kernel(off_ref, q_hbm, k_hbm, v_hbm, w_hbm, grad_hbm,
                 res_hbm, dq_hbm, dk_hbm, dv_hbm, total_hbm,
                 q_ref, k_ref, v_ref, w_ref, grad_ref, g_ref, att_ref, res_ref, dq_ref, dk_ref, dv_ref,
                 kv_sel, q_sel, g_sel, os_sel, kv_all, q_all, g_all, os_all,
                 back_att, back_stat, got_att, got_stat, dkv, dqf, got_dkv, got_dq,
                 near_t, lse_cols, lse_ref, delta_ref, dq_acc, dqn_acc, dk_acc, dv_acc,
                 acc, s0, r0, sbuf, rbuf1, rbuf2, last, total_ref,
                 load_sem, store_sem, far_send, far_recv, send_sem, recv_sem):
    dp = lax.axis_index("dp")
    seq = lax.axis_index("seq")
    my_head, my_part = seq // HOLD, seq % HOLD
    coord = [(seq // st) % 4 for st in STRIDES]
    sibling = (1 - dp, seq)
    barrier = pltpu.get_barrier_semaphore()
    loads = [pltpu.make_async_copy(s, d, load_sem.at[i]) for i, (s, d) in enumerate(
        ((k_hbm, k_ref), (v_hbm, v_ref), (q_hbm, q_ref), (w_hbm, w_ref), (grad_hbm, grad_ref)))]
    for load in loads:
        load.start()
    pl.semaphore_signal(barrier, inc=1, device_id=sibling, device_id_type=MESH)

    moved = [[lax.rem(coord[axis] + d, 4) * STRIDES[axis] for d in range(4)] for axis in range(3)]
    others = [moved[0][a] + moved[1][b] + moved[2][c] for a, b, c in FAR_FIRST]
    for d in others:
        pl.semaphore_signal(barrier, inc=1, device_id=(dp, d), device_id_type=MESH)

    started = []
    stores = []

    def store(src, dst, sem):
        st = pltpu.make_async_copy(src, dst, sem)
        st.start()
        stores.append(st)

    def to_group(src, dst, k):
        @pl.loop(1, HEADS)
        def _(i):
            h = lax.rem(my_head + i, HEADS)
            pltpu.make_async_remote_copy(
                src_ref=src.at[h], dst_ref=dst.at[my_head], send_sem=far_send.at[k], recv_sem=far_recv.at[k],
                device_id=(dp, h * HOLD + my_part), device_id_type=MESH).start()
        dst[my_head] = src[my_head]

    loads[0].wait()
    loads[1].wait()

    for h in range(HEADS):
        s = picker(off_ref[h]).astype(jnp.bfloat16)
        kv_sel[h, 0] = mm(s, k_ref[:, head_cols(h)]).astype(jnp.bfloat16)
        kv_sel[h, 1] = mm(s, v_ref[:, head_cols(h)]).astype(jnp.bfloat16)

    pl.semaphore_wait(barrier, 64)

    for d in others:
        pltpu.make_async_remote_copy(
            src_ref=kv_sel.at[d // HOLD], dst_ref=kv_all.at[:, seq], send_sem=far_send.at[0], recv_sem=far_recv.at[0],
            device_id=(dp, d), device_id_type=MESH).start()

    kv_all[:, seq] = kv_sel[my_head]

    loads[2].wait()

    for h in range(HEADS):
        s = picker(off_ref[h]).astype(jnp.bfloat16)
        q_sel[h] = mm(s, q_ref[:, head_cols(h)]).astype(jnp.bfloat16)

    to_group(q_sel, q_all, 1)

    for h in range(HEADS):
        o, lse = softmax_out(q_sel[h], k_ref[:, head_cols(h)], with_ones(v_ref[:, head_cols(h)]))
        os_sel[h, 0] = o
        os_sel[h, 1] = lse

    to_group(os_sel, os_all, 2)

    loads[3].wait()
    loads[4].wait()

    @pl.loop(0, 4)
    def _(c):
        cols = pl.ds(pl.multiple_of(c * 256, 256), 256)
        g_ref[:, cols] = mm(grad_ref[...], w_ref[cols, :], NT).astype(jnp.bfloat16)

    for h in range(HEADS):
        s = picker(off_ref[h]).astype(jnp.bfloat16)
        g_sel[h] = mm(s, g_ref[:, head_cols(h)]).astype(jnp.bfloat16)

    to_group(g_sel, g_all, 3)

    lse_cols[...] = jnp.zeros_like(lse_cols)

    @pl.loop(0, HEADS)
    def _(h):
        v1 = with_ones(v_ref[:, head_cols(h)])
        k = k_ref[:, head_cols(h)]
        for r in range(2):
            rows = slice(r * 256, r * 256 + 256)
            o, lse = softmax_out(q_ref[rows, head_cols(h)], k, v1)
            near_t[head_cols(h), rows] = o.astype(jnp.bfloat16).T
            lane = lax.broadcasted_iota(jnp.int32, (256, 128), 1)
            lse_cols[rows] = jnp.where(lane == h, lse, lse_cols[rows])

    wait_bytes(q_all.at[pl.ds(0, 7)], far_recv.at[1])
    wait_bytes(kv_all.at[:, pl.ds(0, 63)], far_recv.at[0])
    q = q_all[...].reshape(256, DIM)
    k = kv_all[0].reshape(2048, DIM)
    v1 = with_ones(kv_all[1].reshape(2048, DIM))
    far = [softmax_out(q[r * 128:r * 128 + 128], k, v1) for r in range(2)]
    far_out = jnp.concatenate([f[0] for f in far], axis=0)
    far_lse = jnp.concatenate([f[1] for f in far], axis=0)
    wait_bytes(os_all.at[pl.ds(0, 7)], far_recv.at[2])
    near_sel = os_all[:, 0].reshape(256, DIM)
    near_lse = os_all[:, 1].reshape(256, DIM)
    top = jnp.maximum(near_lse, far_lse)
    mixed = top + jnp.log(jnp.exp2(near_lse - top) + jnp.exp2(far_lse - top)) * LOG2E
    att = (jnp.exp2(near_lse - mixed) * near_sel + jnp.exp2(far_lse - mixed) * far_out).astype(jnp.bfloat16)
    back_att[...] = att.reshape(HOLD, PICK, DIM)
    to_group(back_att, got_att, 4)
    wait_bytes(g_all.at[pl.ds(0, 7)], far_recv.at[3])
    g = g_all[...].reshape(256, DIM)
    delta = jnp.sum(g.astype(jnp.float32) * att.astype(jnp.float32), axis=1, keepdims=True)
    lane = lax.broadcasted_iota(jnp.int32, (256, DIM), 1)
    stat = jnp.where(lane < 64, mixed, delta)
    back_stat[...] = stat.reshape(HOLD, PICK, DIM)
    to_group(back_stat, got_stat, 5)
    stat_t = stat.T
    mixed_lane = stat_t[0:1, :]
    delta_lane = stat_t[64:65, :]
    dq_acc[...] = jnp.zeros_like(dq_acc)

    for c in range(4):
        blocks = pl.ds(c * 16, 16)
        kc = kv_all[0, blocks].reshape(512, DIM)
        vc = kv_all[1, blocks].reshape(512, DIM)
        qq = q_all[...].reshape(256, DIM)
        gg = g_all[...].reshape(256, DIM)
        p = jnp.exp2(mm(kc, qq, NT) * SCALE2 - mixed_lane)
        ds = (p * (mm(vc, gg, NT) - delta_lane)).astype(jnp.bfloat16)
        dkv[0, blocks] = (mm(ds, qq) * SCALE).astype(jnp.bfloat16).reshape(16, PICK, DIM)
        dkv[1, blocks] = mm(p.astype(jnp.bfloat16), gg).astype(jnp.bfloat16).reshape(16, PICK, DIM)
        dq_acc[...] += mm(ds, kc, TN)

    dqf[...] = (dq_acc[...] * SCALE).astype(jnp.bfloat16).reshape(HOLD, PICK, DIM)

    for d in others:
        pltpu.make_async_remote_copy(
            src_ref=dkv.at[:, d], dst_ref=got_dkv.at[seq], send_sem=far_send.at[6], recv_sem=far_recv.at[6],
            device_id=(dp, d), device_id_type=MESH).start()

    got_dkv[seq] = dkv[:, seq]
    to_group(dqf, got_dq, 7)

    wait_bytes(got_att.at[pl.ds(0, 7)], far_recv.at[4])
    lane1 = lax.rem(lax.broadcasted_iota(jnp.int32, (1, TOK), 1), RATE)
    def assemble(core):
        for i in range(4):
            h = core * 4 + i
            rows = pl.ds(pl.multiple_of(h * DIM, DIM), DIM)
            put = mm(got_att[h], picker(off_ref[h]).astype(jnp.bfloat16), TN)
            near_t[rows, :] = jnp.where(lane1 == off_ref[h], put, near_t[rows, :].astype(jnp.float32)).astype(jnp.bfloat16)

    assemble(1 - dp)

    def peer(axis, d):
        c = lax.rem(coord[axis] + d, 4)
        return c, (dp, seq + (c - coord[axis]) * STRIDES[axis])

    def copy(p, k, src, dst, target):
        cp = pltpu.make_async_remote_copy(
            src_ref=src, dst_ref=dst, send_sem=send_sem.at[p, k], recv_sem=recv_sem.at[p, k],
            device_id=target, device_id_type=MESH)
        cp.start()
        started.append(cp)
        return cp

    mine = pl.multiple_of(dp * 512, 512)
    other = pl.multiple_of((1 - dp) * 512, 512)
    first = []
    for p in range(6):
        s0[:, COLS[p]] = mm(near_t[pl.ds(other, 512), :], grad_ref[:, COLS[p]]).astype(jnp.bfloat16)
        first.append(copy(p, 0, s0.at[:, COLS[p]], r0.at[:, COLS[p]], sibling))
    assemble(dp)

    flight = [None] * 6

    def send_rows(p, level, base, n, buf, landing):
        axis = ORDERS[p][level]
        flight[p] = []
        for d in (1, 2, 3):
            c, target = peer(axis, d)
            rows = slice((d - 1) * n, d * n)
            buf[rows, COLS[p]] = acc[pl.ds(pl.multiple_of(base + c * n, n), n), COLS[p]].astype(jnp.bfloat16)
            flight[p].append(copy(p, 1 + 3 * level + d - 1, buf.at[rows, COLS[p]], landing.at[rows, COLS[p]], target))

    base1 = []
    for p in range(6):
        first[p].wait_recv()
        acc[:, COLS[p]] = mm(near_t[pl.ds(mine, 512), :], grad_ref[:, COLS[p]]) + r0[:, COLS[p]].astype(jnp.float32)
        send_rows(p, 0, 0, 128, sbuf, rbuf1)
        base1.append(pl.multiple_of(coord[ORDERS[p][0]] * 128, 128))

    def statistics():
        lse_ref[...] = lse_cols[...].T[0:HEADS, :]
        wait_bytes(got_stat.at[pl.ds(0, 7)], far_recv.at[5])
        for h in range(HEADS):
            pick = picker(off_ref[h])
            st = got_stat[h]
            mixed_h = jnp.sum(jnp.where(pick, st[:, 0:1], 0.0), axis=0, keepdims=True)
            lse_ref[h:h + 1, :] = jnp.where(lane1 == off_ref[h], mixed_h, lse_ref[h:h + 1, :])
            delta_ref[h:h + 1, :] = jnp.sum(jnp.where(pick, st[:, 64:65], 0.0), axis=0, keepdims=True)

    def project(c):
        cs = slice(c * 512, c * 512 + 512)
        res_ref[:, cs] = mm(att_ref[...], w_ref[:, cs]).astype(jnp.bfloat16)
        store(res_ref.at[:, cs], res_hbm.at[:, cs], store_sem.at[0, c])

    def returned():
        wait_bytes(got_dkv.at[pl.ds(0, 63)], far_recv.at[6])
        wait_bytes(got_dq.at[pl.ds(0, 7)], far_recv.at[7])

    def near_back(h):
        hs = slice(h * DIM, h * DIM + DIM)
        off = off_ref[h]
        q, k, g = q_ref[:, hs], k_ref[:, hs], g_ref[:, hs]
        probs = jnp.exp2(mm(k, q, NT) * SCALE2 - lse_ref[h:h + 1, :])
        low = probs.astype(jnp.bfloat16)
        prod = probs * mm(v_ref[:, hs], g, NT)
        delta = jnp.where(lane1 == off, delta_ref[h:h + 1, :], jnp.sum(prod, axis=0, keepdims=True))
        ds = (prod - probs * delta).astype(jnp.bfloat16)
        dv_acc[:, hs] = mm(low, g)
        dk_acc[:, hs] = mm(ds, q) * SCALE
        dqn_acc[:, hs] = mm(ds, k, TN) * SCALE

    def deposit(h):
        hs = slice(h * DIM, h * DIM + DIM)
        off = off_ref[h]
        put = (lax.broadcasted_iota(jnp.int32, (TOK, HOLD * PICK), 0)
               == lax.rem(lax.broadcasted_iota(jnp.int32, (TOK, HOLD * PICK), 1), PICK) * RATE + off).astype(jnp.bfloat16)
        far = slice(h * HOLD, h * HOLD + HOLD)
        dv_ref[:, hs] = (dv_acc[:, hs] + mm(put, got_dkv[far, 1].reshape(HOLD * PICK, DIM))).astype(jnp.bfloat16)
        dk_ref[:, hs] = (dk_acc[:, hs] + mm(put, got_dkv[far, 0].reshape(HOLD * PICK, DIM))).astype(jnp.bfloat16)
        dq_ref[:, hs] = (dqn_acc[:, hs] + mm(put[:, :PICK], got_dq[h])).astype(jnp.bfloat16)
        for i, (a, b) in enumerate(((dq_ref, dq_hbm), (dk_ref, dk_hbm), (dv_ref, dv_hbm))):
            store(a.at[:, hs], b.at[:, hs], store_sem.at[1 + i, h])

    att_ref[...] = near_t[...].T
    for c in range(4):
        project(c)
    statistics()
    near_back(0)
    near_back(1)
    near_back(2)

    def add_received(p, base, n, landing):
        for cp in flight[p]:
            cp.wait_recv()
        rows = pl.ds(pl.multiple_of(base, n), n)
        total = acc[rows, COLS[p]]
        for d in range(3):
            total += landing[d * n:d * n + n, COLS[p]].astype(jnp.float32)
        acc[rows, COLS[p]] = total

    base2 = []
    for p in range(6):
        add_received(p, base1[p], 128, rbuf1)
        send_rows(p, 1, base1[p], 32, sbuf.at[384:480], rbuf2)
        base2.append(pl.multiple_of(base1[p] + coord[ORDERS[p][1]] * 32, 32))
    near_back(3)
    near_back(4)
    for p in range(6):
        add_received(p, base2[p], 32, rbuf2)
        axis = ORDERS[p][2]
        here = coord[axis]
        last[here, :, COLS[p]] = acc[pl.ds(base2[p], 32), COLS[p]].astype(jnp.bfloat16)
        flight[p] = []
        for d in (1, 2, 3):
            _, target = peer(axis, d)
            flight[p].append(copy(p, 6 + d, last.at[here, :, COLS[p]], last.at[here, :, COLS[p]], target))
    near_back(5)
    near_back(6)
    for p in range(6):
        for cp in flight[p]:
            cp.wait_recv()
        total = last[0, :, COLS[p]].astype(jnp.float32)
        for j in (1, 2, 3):
            total += last[j, :, COLS[p]].astype(jnp.float32)
        rows = pl.ds(pl.multiple_of(mine + base2[p], 32), 32)
        total_ref[rows, COLS[p]] = total.astype(jnp.bfloat16)
        block = total_ref.at[rows, COLS[p]]
        flight[p] = [copy(p, 9 + d, block, block, peer(ORDERS[p][1], d)[1]) for d in (1, 2, 3)]
    near_back(7)
    final = []
    for p in range(6):
        for cp in flight[p]:
            cp.wait_recv()
        block = total_ref.at[pl.ds(pl.multiple_of(mine + base1[p], 128), 128), COLS[p]]
        flight[p] = [copy(p, 12 + d, block, block, peer(ORDERS[p][0], d)[1]) for d in (1, 2, 3)]
        final.append(copy(p, 16, block, block, sibling))
    returned()
    for h in range(HEADS):
        deposit(h)
    for p in range(6):
        for d in (1, 2, 3):
            flight[p][d - 1].wait_recv()
            c = lax.rem(coord[ORDERS[p][0]] + 4 - d, 4)
            block = total_ref.at[pl.ds(pl.multiple_of(mine + c * 128, 128), 128), COLS[p]]
            final.append(copy(p, 16 + d, block, block, sibling))
    mine_out = pltpu.make_async_copy(total_ref.at[pl.ds(mine, 512)], total_hbm.at[pl.ds(mine, 512)], load_sem.at[5])
    mine_out.start()
    for cp in final:
        cp.wait_recv()
    other_out = pltpu.make_async_copy(total_ref.at[pl.ds(other, 512)], total_hbm.at[pl.ds(other, 512)], load_sem.at[6])
    other_out.start()
    for cp in started:
        cp.wait_send()
    for st in stores:
        st.wait()
    wait_bytes(kv_all.at[:, pl.ds(0, 63)], far_send.at[0])
    for i, ref in ((1, q_all), (2, os_all), (3, g_all), (4, got_att), (5, got_stat), (7, got_dq)):
        wait_bytes(ref.at[pl.ds(0, 7)], far_send.at[i])
    wait_bytes(got_dkv.at[pl.ds(0, 63)], far_send.at[6])
    mine_out.wait()
    other_out.wait()


def layer_call(offsets, q, k, v, w, grad):
    bf, f32 = jnp.bfloat16, jnp.float32
    hbm = pl.BlockSpec(memory_space=pl.ANY)
    S = jax.ShapeDtypeStruct
    V = pltpu.VMEM
    wide, flat = (TOK, 2048), (TOK, 1024)
    rows = (HEADS, PICK, DIM)
    return pl.pallas_call(
        layer_kernel,
        out_shape=(S(wide, bf), S(flat, bf), S(flat, bf), S(flat, bf), S((1024, 2048), bf)),
        in_specs=[pl.BlockSpec(memory_space=pltpu.SMEM)] + [hbm] * 5,
        out_specs=(hbm,) * 5,
        scratch_shapes=[
            V(flat, bf), V(flat, bf), V(flat, bf), V((1024, 2048), bf), V(wide, bf), V(flat, bf), V(flat, bf),
            V(wide, bf), V(flat, bf), V(flat, bf), V(flat, bf),
            V((HEADS, 2, PICK, DIM), bf), V(rows, bf), V(rows, bf), V((HEADS, 2, PICK, DIM), f32),
            V((2, 64, PICK, DIM), bf), V(rows, bf), V(rows, bf), V((HOLD, 2, PICK, DIM), f32),
            V(rows, bf), V(rows, f32), V(rows, bf), V(rows, f32),
            V((2, 64, PICK, DIM), bf), V(rows, bf), V((64, 2, PICK, DIM), bf), V(rows, bf),
            V((1024, TOK), bf), V((TOK, 128), f32), V((HEADS, TOK), f32), V((HEADS, TOK), f32), V((256, DIM), f32),
            V(flat, f32), V(flat, f32), V(flat, f32),
            V(wide, f32), V(wide, bf), V(wide, bf), V(wide, bf), V((384, 2048), bf), V((96, 2048), bf),
            V((4, 32, 2048), bf), V((1024, 2048), bf),
            pltpu.SemaphoreType.DMA((7,)), pltpu.SemaphoreType.DMA((4, 8)),
            pltpu.SemaphoreType.DMA((8,)), pltpu.SemaphoreType.DMA((8,)),
            pltpu.SemaphoreType.DMA((6, 20)), pltpu.SemaphoreType.DMA((6, 20)),
        ],
        compiler_params=pltpu.CompilerParams(collective_id=0, has_side_effects=True, vmem_limit_bytes=60 * 1024 * 1024),
    )(offsets, q, k, v, w, grad)


def finish_kernel(scale, total_hbm, res_hbm, dq_hbm, dk_hbm, dv_hbm, wg_out, res_out, dq_out, dk_out, dv_out,
                  low, wide, res_ref, dq_ref, dk_ref, dv_ref, copy_sem, in_sem, out_sem):
    pieces = [slice(i * 128, i * 128 + 128) for i in range(8)]
    ins = [pltpu.make_async_copy(total_hbm.at[rows], low.at[rows], in_sem.at[i]) for i, rows in enumerate(pieces)]
    for cp in ins:
        cp.start()
    rest = ((res_hbm, res_ref, res_out), (dq_hbm, dq_ref, dq_out), (dk_hbm, dk_ref, dk_out), (dv_hbm, dv_ref, dv_out))
    copies = [pltpu.make_async_copy(a, b, copy_sem.at[0, i]) for i, (a, b, _) in enumerate(rest)]
    for cp in copies:
        cp.start()
    outs = []
    for i, rows in enumerate(pieces):
        ins[i].wait()
        wide[rows] = low[rows].astype(jnp.float32) * scale
        outs.append(pltpu.make_async_copy(wide.at[rows], wg_out.at[rows], out_sem.at[i]))
        outs[-1].start()
    for i, (_, b, c) in enumerate(rest):
        copies[i].wait()
        outs.append(pltpu.make_async_copy(b, c, copy_sem.at[1, i]))
        outs[-1].start()
    for cp in outs:
        cp.wait()


def finish_call(total, res, dq, dk, dv):
    bf = jnp.bfloat16
    hbm = pl.BlockSpec(memory_space=pl.ANY)
    S = jax.ShapeDtypeStruct
    flat = S((TOK, 1024), bf)

    def kernel(*refs):
        finish_kernel(1.0 / math.sqrt(65536), *refs)

    return pl.pallas_call(
        kernel,
        out_shape=(S((1024, 2048), jnp.float32), S((TOK, 2048), bf), flat, flat, flat),
        in_specs=[hbm] * 5,
        out_specs=(hbm,) * 5,
        scratch_shapes=[pltpu.VMEM((1024, 2048), bf), pltpu.VMEM((1024, 2048), jnp.float32),
                        pltpu.VMEM((TOK, 2048), bf), pltpu.VMEM((TOK, 1024), bf), pltpu.VMEM((TOK, 1024), bf),
                        pltpu.VMEM((TOK, 1024), bf), pltpu.SemaphoreType.DMA((2, 4)), pltpu.SemaphoreType.DMA((8,)), pltpu.SemaphoreType.DMA((8,))],
        compiler_params=pltpu.CompilerParams(vmem_limit_bytes=60 * 1024 * 1024),
    )(total, res, dq, dk, dv)


def per_device(queries, keys, values, offsets, out_weight, grad_out):
    res, dq, dk, dv, total = layer_call(offsets, queries[0], keys[0], values[0], out_weight, grad_out[0])
    weight_grad, res, dq, dk, dv = finish_call(total, res, dq, dk, dv)
    return res[None], dq[None], dk[None], dv[None], weight_grad


def solution(mesh):
    split = P("dp", "seq", None)
    return jax.shard_map(
        per_device, mesh=mesh, in_specs=(split, split, split, P(), P(), split),
        out_specs=(split, split, split, split, P()), check_vma=False)
```

```python
import math

import jax
import jax.numpy as jnp
from jax import lax
from jax.experimental import pallas as pl
from jax.experimental.pallas import tpu as pltpu
from jax.sharding import PartitionSpec as P

MESH = pl.DeviceIdType.MESH

RATE = 16
HEADS = 8
DIM = 128
TOK = 512
PICK = 32
HOLD = 8
SCALE = DIM ** -0.5
LOG2E = math.log2(math.e)
SCALE2 = SCALE * LOG2E
NT = (((1,), (1,)), ((), ()))
TN = (((0,), (0,)), ((), ()))


def mm(a, b, dims=(((1,), (0,)), ((), ()))):
    return lax.dot_general(a, b, dims, preferred_element_type=jnp.float32)


def head_cols(h):
    if isinstance(h, int):
        return slice(h * DIM, h * DIM + DIM)
    return pl.ds(pl.multiple_of(h * DIM, DIM), DIM)


def picker(off):
    row = lax.broadcasted_iota(jnp.int32, (PICK, TOK), 0)
    pos = lax.broadcasted_iota(jnp.int32, (PICK, TOK), 1)
    return pos == row * RATE + off


def with_ones(value):
    return jnp.concatenate([value, jnp.ones_like(value)], axis=1)


def softmax_out(q, k, v1):
    s = mm(q, k, NT)
    top = jnp.max(s, axis=1, keepdims=True) * SCALE2
    e = jnp.exp2(s * SCALE2 - top).astype(jnp.bfloat16)
    ov = mm(e, v1)
    total = ov[:, DIM:]
    return ov[:, :DIM] / total, top + jnp.log(total) * LOG2E


def split3(x):
    high = x.astype(jnp.bfloat16).astype(jnp.float32)
    mid = (x - high).astype(jnp.bfloat16).astype(jnp.float32)
    lane = lax.broadcasted_iota(jnp.int32, x.shape, 1)
    return jnp.where(lane < 32, high, jnp.where(lane < 64, mid, x - high - mid)).astype(jnp.bfloat16)


def join3(code, at):
    x = code.astype(jnp.float32)
    return x[:, at:at + 1] + x[:, at + 32:at + 33] + x[:, at + 64:at + 65]


def wait_bytes(ref, sem):
    pltpu.make_async_copy(ref, ref, sem).wait()


STRIDES = (16, 4, 1)
WIDTHS = (384, 384, 384, 384, 256, 256)
STARTS = (0, 384, 768, 1152, 1536, 1792)
COLS = [slice(a, a + b) for a, b in zip(STARTS, WIDTHS)]
ORDERS = ((0, 1, 2), (1, 2, 0), (2, 0, 1)) * 2
FAR_FIRST = sorted(((a, b, c) for a in range(4) for b in range(4) for c in range(4) if a + b + c > 0),
                   key=lambda o: -sum(min(d, 4 - d) for d in o))


def layer_kernel(off_ref, q_hbm, k_hbm, v_hbm, w_hbm, grad_hbm,
                 res_hbm, dq_hbm, dk_hbm, dv_hbm, total_hbm,
                 q_ref, k_ref, v_ref, w_ref, grad_ref, g_ref, att_ref, res_ref, dq_ref, dk_ref, dv_ref,
                 kv_sel, q_sel, g_sel, os_sel, kv_all, q_all, g_all, os_all,
                 back_att, back_stat, got_att, got_stat, dkv, dqf, got_dkv, got_dq,
                 near_t, lse_cols, lse_ref, delta_ref, dq_acc, dqn_acc, dk_acc, dv_acc,
                 acc, s0, r0, sbuf, rbuf1, rbuf2, last, total_ref,
                 load_sem, store_sem, far_send, far_recv, send_sem, recv_sem):
    dp = lax.axis_index("dp")
    seq = lax.axis_index("seq")
    my_head, my_part = seq // HOLD, seq % HOLD
    coord = [(seq // st) % 4 for st in STRIDES]
    sibling = (1 - dp, seq)
    barrier = pltpu.get_barrier_semaphore()
    loads = [pltpu.make_async_copy(s, d, load_sem.at[i]) for i, (s, d) in enumerate(
        ((k_hbm, k_ref), (v_hbm, v_ref), (q_hbm, q_ref), (w_hbm, w_ref), (grad_hbm, grad_ref)))]
    for load in loads:
        load.start()
    pl.semaphore_signal(barrier, inc=1, device_id=sibling, device_id_type=MESH)

    moved = [[lax.rem(coord[axis] + d, 4) * STRIDES[axis] for d in range(4)] for axis in range(3)]
    others = [moved[0][a] + moved[1][b] + moved[2][c] for a, b, c in FAR_FIRST]
    for d in others:
        pl.semaphore_signal(barrier, inc=1, device_id=(dp, d), device_id_type=MESH)

    started = []
    stores = []

    def store(src, dst, sem):
        st = pltpu.make_async_copy(src, dst, sem)
        st.start()
        stores.append(st)

    def to_group(src, dst, k):
        @pl.loop(1, HEADS)
        def _(i):
            h = lax.rem(my_head + i, HEADS)
            pltpu.make_async_remote_copy(
                src_ref=src.at[h], dst_ref=dst.at[my_head], send_sem=far_send.at[k], recv_sem=far_recv.at[k],
                device_id=(dp, h * HOLD + my_part), device_id_type=MESH).start()
        dst[my_head] = src[my_head]

    loads[0].wait()
    loads[1].wait()

    for h in range(HEADS):
        s = picker(off_ref[h]).astype(jnp.bfloat16)
        kv_sel[h, 0] = mm(s, k_ref[:, head_cols(h)]).astype(jnp.bfloat16)
        kv_sel[h, 1] = mm(s, v_ref[:, head_cols(h)]).astype(jnp.bfloat16)

    pl.semaphore_wait(barrier, 64)

    for d in others:
        pltpu.make_async_remote_copy(
            src_ref=kv_sel.at[d // HOLD], dst_ref=kv_all.at[:, seq], send_sem=far_send.at[0], recv_sem=far_recv.at[0],
            device_id=(dp, d), device_id_type=MESH).start()

    kv_all[:, seq] = kv_sel[my_head]

    loads[2].wait()

    for h in range(HEADS):
        s = picker(off_ref[h]).astype(jnp.bfloat16)
        q_sel[h] = mm(s, q_ref[:, head_cols(h)]).astype(jnp.bfloat16)

    to_group(q_sel, q_all, 1)

    for h in range(HEADS):
        o, lse = softmax_out(q_sel[h], k_ref[:, head_cols(h)], with_ones(v_ref[:, head_cols(h)]))
        os_sel[h, 0] = o.astype(jnp.bfloat16)
        os_sel[h, 1] = split3(lse)

    to_group(os_sel, os_all, 2)

    loads[3].wait()
    loads[4].wait()

    @pl.loop(0, 4)
    def _(c):
        cols = pl.ds(pl.multiple_of(c * 256, 256), 256)
        g_ref[:, cols] = mm(grad_ref[...], w_ref[cols, :], NT).astype(jnp.bfloat16)

    for h in range(HEADS):
        s = picker(off_ref[h]).astype(jnp.bfloat16)
        g_sel[h] = mm(s, g_ref[:, head_cols(h)]).astype(jnp.bfloat16)

    to_group(g_sel, g_all, 3)

    lse_cols[...] = jnp.zeros_like(lse_cols)

    @pl.loop(0, HEADS)
    def _(h):
        v1 = with_ones(v_ref[:, head_cols(h)])
        k = k_ref[:, head_cols(h)]
        for r in range(2):
            rows = slice(r * 256, r * 256 + 256)
            o, lse = softmax_out(q_ref[rows, head_cols(h)], k, v1)
            near_t[head_cols(h), rows] = o.astype(jnp.bfloat16).T
            lane = lax.broadcasted_iota(jnp.int32, (256, 128), 1)
            lse_cols[rows] = jnp.where(lane == h, lse, lse_cols[rows])

    wait_bytes(q_all.at[pl.ds(0, 7)], far_recv.at[1])
    wait_bytes(kv_all.at[:, pl.ds(0, 63)], far_recv.at[0])
    q = q_all[...].reshape(256, DIM)
    k = kv_all[0].reshape(2048, DIM)
    v1 = with_ones(kv_all[1].reshape(2048, DIM))
    far = [softmax_out(q[r * 128:r * 128 + 128], k, v1) for r in range(2)]
    far_out = jnp.concatenate([f[0] for f in far], axis=0)
    far_lse = jnp.concatenate([f[1] for f in far], axis=0)
    wait_bytes(os_all.at[pl.ds(0, 7)], far_recv.at[2])
    near_sel = os_all[:, 0].reshape(256, DIM).astype(jnp.float32)
    near_lse = join3(os_all[:, 1].reshape(256, DIM), 0)
    top = jnp.maximum(near_lse, far_lse)
    mixed = top + jnp.log(jnp.exp2(near_lse - top) + jnp.exp2(far_lse - top)) * LOG2E
    att = (jnp.exp2(near_lse - mixed) * near_sel + jnp.exp2(far_lse - mixed) * far_out).astype(jnp.bfloat16)
    back_att[...] = att.reshape(HOLD, PICK, DIM)
    to_group(back_att, got_att, 4)
    wait_bytes(g_all.at[pl.ds(0, 7)], far_recv.at[3])
    g = g_all[...].reshape(256, DIM)
    delta = jnp.sum(g.astype(jnp.float32) * att.astype(jnp.float32), axis=1, keepdims=True)
    lane = lax.broadcasted_iota(jnp.int32, (256, DIM), 1)
    stat = jnp.where(lane < 64, mixed, delta)
    back_stat[...] = split3(jnp.where(lax.rem(lane, 32) < 16, mixed, delta)).reshape(HOLD, PICK, DIM)
    to_group(back_stat, got_stat, 5)
    stat_t = stat.T
    mixed_lane = stat_t[0:1, :]
    delta_lane = stat_t[64:65, :]
    dq_acc[...] = jnp.zeros_like(dq_acc)

    for c in range(4):
        blocks = pl.ds(c * 16, 16)
        kc = kv_all[0, blocks].reshape(512, DIM)
        vc = kv_all[1, blocks].reshape(512, DIM)
        qq = q_all[...].reshape(256, DIM)
        gg = g_all[...].reshape(256, DIM)
        p = jnp.exp2(mm(kc, qq, NT) * SCALE2 - mixed_lane)
        ds = (p * (mm(vc, gg, NT) - delta_lane)).astype(jnp.bfloat16)
        dkv[0, blocks] = (mm(ds, qq) * SCALE).astype(jnp.bfloat16).reshape(16, PICK, DIM)
        dkv[1, blocks] = mm(p.astype(jnp.bfloat16), gg).astype(jnp.bfloat16).reshape(16, PICK, DIM)
        dq_acc[...] += mm(ds, kc, TN)

    dqf[...] = (dq_acc[...] * SCALE).astype(jnp.bfloat16).reshape(HOLD, PICK, DIM)

    for d in others:
        pltpu.make_async_remote_copy(
            src_ref=dkv.at[:, d], dst_ref=got_dkv.at[seq], send_sem=far_send.at[6], recv_sem=far_recv.at[6],
            device_id=(dp, d), device_id_type=MESH).start()

    got_dkv[seq] = dkv[:, seq]
    to_group(dqf, got_dq, 7)

    wait_bytes(got_att.at[pl.ds(0, 7)], far_recv.at[4])
    lane1 = lax.rem(lax.broadcasted_iota(jnp.int32, (1, TOK), 1), RATE)
    def assemble(core):
        for i in range(4):
            h = core * 4 + i
            rows = pl.ds(pl.multiple_of(h * DIM, DIM), DIM)
            put = mm(got_att[h], picker(off_ref[h]).astype(jnp.bfloat16), TN)
            near_t[rows, :] = jnp.where(lane1 == off_ref[h], put, near_t[rows, :].astype(jnp.float32)).astype(jnp.bfloat16)

    assemble(1 - dp)

    def peer(axis, d):
        c = lax.rem(coord[axis] + d, 4)
        return c, (dp, seq + (c - coord[axis]) * STRIDES[axis])

    def copy(p, k, src, dst, target):
        cp = pltpu.make_async_remote_copy(
            src_ref=src, dst_ref=dst, send_sem=send_sem.at[p, k], recv_sem=recv_sem.at[p, k],
            device_id=target, device_id_type=MESH)
        cp.start()
        started.append(cp)
        return cp

    mine = pl.multiple_of(dp * 512, 512)
    other = pl.multiple_of((1 - dp) * 512, 512)
    first = []
    for p in range(6):
        s0[:, COLS[p]] = mm(near_t[pl.ds(other, 512), :], grad_ref[:, COLS[p]]).astype(jnp.bfloat16)
        first.append(copy(p, 0, s0.at[:, COLS[p]], r0.at[:, COLS[p]], sibling))
    assemble(dp)

    flight = [None] * 6

    def send_rows(p, level, base, n, buf, landing):
        axis = ORDERS[p][level]
        flight[p] = []
        for d in (1, 2, 3):
            c, target = peer(axis, d)
            rows = slice((d - 1) * n, d * n)
            buf[rows, COLS[p]] = acc[pl.ds(pl.multiple_of(base + c * n, n), n), COLS[p]].astype(jnp.bfloat16)
            flight[p].append(copy(p, 1 + 3 * level + d - 1, buf.at[rows, COLS[p]], landing.at[rows, COLS[p]], target))

    base1 = []
    for p in range(6):
        first[p].wait_recv()
        acc[:, COLS[p]] = mm(near_t[pl.ds(mine, 512), :], grad_ref[:, COLS[p]]) + r0[:, COLS[p]].astype(jnp.float32)
        send_rows(p, 0, 0, 128, sbuf, rbuf1)
        base1.append(pl.multiple_of(coord[ORDERS[p][0]] * 128, 128))

    def statistics():
        lse_ref[...] = lse_cols[...].T[0:HEADS, :]
        wait_bytes(got_stat.at[pl.ds(0, 7)], far_recv.at[5])
        for h in range(HEADS):
            pick = picker(off_ref[h])
            st = got_stat[h]
            mixed_h = jnp.sum(jnp.where(pick, join3(st, 0), 0.0), axis=0, keepdims=True)
            lse_ref[h:h + 1, :] = jnp.where(lane1 == off_ref[h], mixed_h, lse_ref[h:h + 1, :])
            delta_ref[h:h + 1, :] = jnp.sum(jnp.where(pick, join3(st, 16), 0.0), axis=0, keepdims=True)

    def project(c):
        cs = slice(c * 512, c * 512 + 512)
        res_ref[:, cs] = mm(att_ref[...], w_ref[:, cs]).astype(jnp.bfloat16)
        store(res_ref.at[:, cs], res_hbm.at[:, cs], store_sem.at[0, c])

    def returned():
        wait_bytes(got_dkv.at[pl.ds(0, 63)], far_recv.at[6])
        wait_bytes(got_dq.at[pl.ds(0, 7)], far_recv.at[7])

    def near_back(h):
        hs = slice(h * DIM, h * DIM + DIM)
        off = off_ref[h]
        q, k, g = q_ref[:, hs], k_ref[:, hs], g_ref[:, hs]
        probs = jnp.exp2(mm(k, q, NT) * SCALE2 - lse_ref[h:h + 1, :])
        low = probs.astype(jnp.bfloat16)
        prod = probs * mm(v_ref[:, hs], g, NT)
        delta = jnp.where(lane1 == off, delta_ref[h:h + 1, :], jnp.sum(prod, axis=0, keepdims=True))
        ds = (prod - probs * delta).astype(jnp.bfloat16)
        dv_acc[:, hs] = mm(low, g)
        dk_acc[:, hs] = mm(ds, q) * SCALE
        dqn_acc[:, hs] = mm(ds, k, TN) * SCALE

    def deposit(h):
        hs = slice(h * DIM, h * DIM + DIM)
        off = off_ref[h]
        put = (lax.broadcasted_iota(jnp.int32, (TOK, HOLD * PICK), 0)
               == lax.rem(lax.broadcasted_iota(jnp.int32, (TOK, HOLD * PICK), 1), PICK) * RATE + off).astype(jnp.bfloat16)
        far = slice(h * HOLD, h * HOLD + HOLD)
        dv_ref[:, hs] = (dv_acc[:, hs] + mm(put, got_dkv[far, 1].reshape(HOLD * PICK, DIM))).astype(jnp.bfloat16)
        dk_ref[:, hs] = (dk_acc[:, hs] + mm(put, got_dkv[far, 0].reshape(HOLD * PICK, DIM))).astype(jnp.bfloat16)
        dq_ref[:, hs] = (dqn_acc[:, hs] + mm(put[:, :PICK], got_dq[h])).astype(jnp.bfloat16)
        for i, (a, b) in enumerate(((dq_ref, dq_hbm), (dk_ref, dk_hbm), (dv_ref, dv_hbm))):
            store(a.at[:, hs], b.at[:, hs], store_sem.at[1 + i, h])

    att_ref[...] = near_t[...].T
    for c in range(4):
        project(c)
    statistics()
    near_back(0)
    near_back(1)
    near_back(2)

    def add_received(p, base, n, landing):
        for cp in flight[p]:
            cp.wait_recv()
        rows = pl.ds(pl.multiple_of(base, n), n)
        total = acc[rows, COLS[p]]
        for d in range(3):
            total += landing[d * n:d * n + n, COLS[p]].astype(jnp.float32)
        acc[rows, COLS[p]] = total

    base2 = []
    for p in range(6):
        add_received(p, base1[p], 128, rbuf1)
        send_rows(p, 1, base1[p], 32, sbuf.at[384:480], rbuf2)
        base2.append(pl.multiple_of(base1[p] + coord[ORDERS[p][1]] * 32, 32))
    near_back(3)
    near_back(4)
    for p in range(6):
        add_received(p, base2[p], 32, rbuf2)
        axis = ORDERS[p][2]
        here = coord[axis]
        last[here, :, COLS[p]] = acc[pl.ds(base2[p], 32), COLS[p]].astype(jnp.bfloat16)
        flight[p] = []
        for d in (1, 2, 3):
            _, target = peer(axis, d)
            flight[p].append(copy(p, 6 + d, last.at[here, :, COLS[p]], last.at[here, :, COLS[p]], target))
    near_back(5)
    near_back(6)
    for p in range(6):
        for cp in flight[p]:
            cp.wait_recv()
        total = last[0, :, COLS[p]].astype(jnp.float32)
        for j in (1, 2, 3):
            total += last[j, :, COLS[p]].astype(jnp.float32)
        rows = pl.ds(pl.multiple_of(mine + base2[p], 32), 32)
        total_ref[rows, COLS[p]] = total.astype(jnp.bfloat16)
        block = total_ref.at[rows, COLS[p]]
        flight[p] = [copy(p, 9 + d, block, block, peer(ORDERS[p][1], d)[1]) for d in (1, 2, 3)]
    near_back(7)
    final = []
    for p in range(6):
        for cp in flight[p]:
            cp.wait_recv()
        block = total_ref.at[pl.ds(pl.multiple_of(mine + base1[p], 128), 128), COLS[p]]
        flight[p] = [copy(p, 12 + d, block, block, peer(ORDERS[p][0], d)[1]) for d in (1, 2, 3)]
        final.append(copy(p, 16, block, block, sibling))
    returned()
    for h in range(HEADS):
        deposit(h)
    for p in range(6):
        for d in (1, 2, 3):
            flight[p][d - 1].wait_recv()
            c = lax.rem(coord[ORDERS[p][0]] + 4 - d, 4)
            block = total_ref.at[pl.ds(pl.multiple_of(mine + c * 128, 128), 128), COLS[p]]
            final.append(copy(p, 16 + d, block, block, sibling))
    mine_out = pltpu.make_async_copy(total_ref.at[pl.ds(mine, 512)], total_hbm.at[pl.ds(mine, 512)], load_sem.at[5])
    mine_out.start()
    for cp in final:
        cp.wait_recv()
    other_out = pltpu.make_async_copy(total_ref.at[pl.ds(other, 512)], total_hbm.at[pl.ds(other, 512)], load_sem.at[6])
    other_out.start()
    for cp in started:
        cp.wait_send()
    for st in stores:
        st.wait()
    wait_bytes(kv_all.at[:, pl.ds(0, 63)], far_send.at[0])
    for i, ref in ((1, q_all), (2, os_all), (3, g_all), (4, got_att), (5, got_stat), (7, got_dq)):
        wait_bytes(ref.at[pl.ds(0, 7)], far_send.at[i])
    wait_bytes(got_dkv.at[pl.ds(0, 63)], far_send.at[6])
    mine_out.wait()
    other_out.wait()


def layer_call(offsets, q, k, v, w, grad):
    bf, f32 = jnp.bfloat16, jnp.float32
    hbm = pl.BlockSpec(memory_space=pl.ANY)
    S = jax.ShapeDtypeStruct
    V = pltpu.VMEM
    wide, flat = (TOK, 2048), (TOK, 1024)
    rows = (HEADS, PICK, DIM)
    return pl.pallas_call(
        layer_kernel,
        out_shape=(S(wide, bf), S(flat, bf), S(flat, bf), S(flat, bf), S((1024, 2048), bf)),
        in_specs=[pl.BlockSpec(memory_space=pltpu.SMEM)] + [hbm] * 5,
        out_specs=(hbm,) * 5,
        scratch_shapes=[
            V(flat, bf), V(flat, bf), V(flat, bf), V((1024, 2048), bf), V(wide, bf), V(flat, bf), V(flat, bf),
            V(wide, bf), V(flat, bf), V(flat, bf), V(flat, bf),
            V((HEADS, 2, PICK, DIM), bf), V(rows, bf), V(rows, bf), V((HEADS, 2, PICK, DIM), bf),
            V((2, 64, PICK, DIM), bf), V(rows, bf), V(rows, bf), V((HOLD, 2, PICK, DIM), bf),
            V(rows, bf), V(rows, bf), V(rows, bf), V(rows, bf),
            V((2, 64, PICK, DIM), bf), V(rows, bf), V((64, 2, PICK, DIM), bf), V(rows, bf),
            V((1024, TOK), bf), V((TOK, 128), f32), V((HEADS, TOK), f32), V((HEADS, TOK), f32), V((256, DIM), f32),
            V(flat, f32), V(flat, f32), V(flat, f32),
            V(wide, f32), V(wide, bf), V(wide, bf), V(wide, bf), V((384, 2048), bf), V((96, 2048), bf),
            V((4, 32, 2048), bf), V((1024, 2048), bf),
            pltpu.SemaphoreType.DMA((7,)), pltpu.SemaphoreType.DMA((4, 8)),
            pltpu.SemaphoreType.DMA((8,)), pltpu.SemaphoreType.DMA((8,)),
            pltpu.SemaphoreType.DMA((6, 20)), pltpu.SemaphoreType.DMA((6, 20)),
        ],
        compiler_params=pltpu.CompilerParams(collective_id=0, has_side_effects=True, vmem_limit_bytes=60 * 1024 * 1024),
    )(offsets, q, k, v, w, grad)


def finish_kernel(scale, total_hbm, res_hbm, dq_hbm, dk_hbm, dv_hbm, wg_out, res_out, dq_out, dk_out, dv_out,
                  low, wide, res_ref, dq_ref, dk_ref, dv_ref, copy_sem, in_sem, out_sem):
    pieces = [slice(i * 128, i * 128 + 128) for i in range(8)]
    ins = [pltpu.make_async_copy(total_hbm.at[rows], low.at[rows], in_sem.at[i]) for i, rows in enumerate(pieces)]
    for cp in ins:
        cp.start()
    rest = ((res_hbm, res_ref, res_out), (dq_hbm, dq_ref, dq_out), (dk_hbm, dk_ref, dk_out), (dv_hbm, dv_ref, dv_out))
    copies = [pltpu.make_async_copy(a, b, copy_sem.at[0, i]) for i, (a, b, _) in enumerate(rest)]
    for cp in copies:
        cp.start()
    outs = []
    for i, rows in enumerate(pieces):
        ins[i].wait()
        wide[rows] = low[rows].astype(jnp.float32) * scale
        outs.append(pltpu.make_async_copy(wide.at[rows], wg_out.at[rows], out_sem.at[i]))
        outs[-1].start()
    for i, (_, b, c) in enumerate(rest):
        copies[i].wait()
        outs.append(pltpu.make_async_copy(b, c, copy_sem.at[1, i]))
        outs[-1].start()
    for cp in outs:
        cp.wait()


def finish_call(total, res, dq, dk, dv):
    bf = jnp.bfloat16
    hbm = pl.BlockSpec(memory_space=pl.ANY)
    S = jax.ShapeDtypeStruct
    flat = S((TOK, 1024), bf)

    def kernel(*refs):
        finish_kernel(1.0 / math.sqrt(65536), *refs)

    return pl.pallas_call(
        kernel,
        out_shape=(S((1024, 2048), jnp.float32), S((TOK, 2048), bf), flat, flat, flat),
        in_specs=[hbm] * 5,
        out_specs=(hbm,) * 5,
        scratch_shapes=[pltpu.VMEM((1024, 2048), bf), pltpu.VMEM((1024, 2048), jnp.float32),
                        pltpu.VMEM((TOK, 2048), bf), pltpu.VMEM((TOK, 1024), bf), pltpu.VMEM((TOK, 1024), bf),
                        pltpu.VMEM((TOK, 1024), bf), pltpu.SemaphoreType.DMA((2, 4)), pltpu.SemaphoreType.DMA((8,)), pltpu.SemaphoreType.DMA((8,))],
        compiler_params=pltpu.CompilerParams(vmem_limit_bytes=60 * 1024 * 1024),
    )(total, res, dq, dk, dv)


def per_device(queries, keys, values, offsets, out_weight, grad_out):
    res, dq, dk, dv, total = layer_call(offsets, queries[0], keys[0], values[0], out_weight, grad_out[0])
    weight_grad, res, dq, dk, dv = finish_call(total, res, dq, dk, dv)
    return res[None], dq[None], dk[None], dv[None], weight_grad


def solution(mesh):
    split = P("dp", "seq", None)
    return jax.shard_map(
        per_device, mesh=mesh, in_specs=(split, split, split, P(), P(), split),
        out_specs=(split, split, split, split, P()), check_vma=False)
```
